32 devices in a mesh: groups: 2 (over y), pairs: 4 (over z), section: 2 (over core), sub: 2 (over x).
Axes of the slice: x: 2, y: 2, z: 4, core: 2. Of those that a mesh axis runs over, the one named last changes fastest.
Arguments:
- raw_record: bfloat16 [64, 49152], P(('groups', 'pairs', 'section'), 'sub'), parts along dimension 0, may hold values from -6 to 6
- fir_taps: float32 [64], replicated, may hold values from -0.75 to 0.75
- channel_ids: int32 [64], P('groups'), parts along dimension 0, may hold values from 0 to 31, each once
- offsets: int32 [8], P(('groups', 'sub')), parts along dimension 0, may hold values from 0 to 16324
- pair_table: int32 [32, 2], P('groups'), parts along dimension 0, may hold values from -1 to 3, as said below
Outputs:
- correlations: float32 [8, 32, 8, 2048], P(('section', 'sub'), ('groups', 'pairs')), parts along dimension 1
The draws below stay inside these ranges and needn't reach their ends.
There are 2 independent parts, one for each index of `groups`. The reference program is written for one: setup_inputs(seed, part) draws one part's arguments, and reference() takes and returns one part's arrays. A program takes and returns all parts, laid end to end along the dimension named above; an argument that names none is the same for every part. Nothing has to cross between parts.
Inputs may be any that keep to these rules, and one draw needn't show every extreme that they name: `pair_table`: each row is a pair block (I, J) with I <= J, or (-1, -1) for an empty slot. Every pair block of the 4 x 4 triangle stands in exactly one slot; all live slots of one owner share the first block I; owners p and p + 2 together hold exactly 5 pair blocks; some owner fills all 4 slots.
All inputs are finite; a program needn't handle non-finite values.
Results may differ from the reference program's by a relative error of at most 0.0075.
Values may be sent and summed in bfloat16 or wider, within the bound.
No kernel may reach another device: no remote copies, remote signals or barrier semaphores. Data moves between devices by JAX's collectives and lax.ppermute only.
A program may use at most 128 MiB of HBM per device.

```python
import math
import jax
import jax.numpy as jnp
from jax import lax

NF = 2048
TAPS = 64
DEC = 4
BAND = 64
NSUB_DEV = 2
SPAN = 24576
NSUB = 4
CH = 32
BLK = 8
CB = 4
SLOTS = 4
N_PAIRS = 4
N_SUB = 2


def draw_pair_table(key, part):
    half_pairs = N_PAIRS // 2
    key_rows, key_flip, key_slots = jax.random.split(key, 3)
    row_pairs = jax.random.permutation(key_rows, half_pairs).astype(jnp.int32)
    flipped = jax.random.randint(key_flip, (half_pairs,), 0, 2).astype(jnp.int32)
    chip_index = jnp.arange(N_PAIRS, dtype=jnp.int32)
    column = chip_index % half_pairs
    low_row = row_pairs[column]
    is_upper = chip_index // half_pairs
    block_row = jnp.where(is_upper == flipped[column], low_row, CB - 1 - low_row)
    scores = jax.random.randint(key_slots, (N_PAIRS, SLOTS), 0, 1 << 20).astype(jnp.int32) * SLOTS + jnp.arange(SLOTS, dtype=jnp.int32)[None, :]
    entry_at_slot = jnp.argsort(scores, axis=1).astype(jnp.int32)
    live_count = CB - block_row
    live_entry = entry_at_slot < live_count[:, None]
    first_block = jnp.where(live_entry, block_row[:, None], -1)
    second_block = jnp.where(live_entry, block_row[:, None] + entry_at_slot, -1)
    return jnp.stack([first_block, second_block], axis=-1).reshape(N_PAIRS * SLOTS, 2).astype(jnp.int32)


def place_ends(values, stream_key, low, top_value):
    shape = values.shape
    place = [jax.random.randint(jax.random.fold_in(stream_key, axis), (), 0, shape[axis]) for axis in range(len(shape))]
    values = values.at[tuple(place)].set(low)
    longest = shape.index(max(shape))
    place[longest] = (place[longest] + 1) % shape[longest]
    return values.at[tuple(place)].set(top_value)


def block_levels(stream_key, shape, pieces, least, top_value):
    factor_of = 1.0
    for dim, blocks in pieces:
        steps = jax.random.uniform(jax.random.fold_in(jax.random.fold_in(stream_key, 6), dim), (blocks,), jnp.float32, least / len(pieces), top_value / len(pieces))
        factor_of = factor_of * jnp.repeat(jnp.exp(steps), shape[dim] // blocks).reshape((-1,) + (1,) * (len(shape) - 1 - dim))
    return factor_of


def centred(key, shape, deviation, reach, pieces=(), kind=jnp.bfloat16):
    level = block_levels(key, shape, pieces, -0.22, 0.18) if pieces else 1.0
    entries = jax.random.normal(key, shape, jnp.float32) * deviation * level
    return jnp.minimum(jnp.maximum(entries, -reach), reach).astype(kind)


def setup_inputs(seed: int = 0, part: int = 0) -> dict:
    arg_keys = jax.random.split(jax.random.key(seed), 6)
    part_keys = jax.random.split(jax.random.fold_in(arg_keys[5], part), 6)
    raw_record = centred(part_keys[0], (CH, N_SUB * SPAN), 1.0, 6.0, ((0, 8), (1, 2)))
    fir_taps = centred(arg_keys[1], (TAPS,), TAPS ** -0.5, 0.75, (), jnp.float32)
    channel_ids = jax.random.permutation(part_keys[2], CH).astype(jnp.int32)
    offsets = place_ends(jax.random.randint(part_keys[3], (NSUB,), 0, SPAN - DEC * (NF - 1) - TAPS + 1), jax.random.fold_in(part_keys[3], 1), 0, SPAN - DEC * (NF - 1) - TAPS).astype(jnp.int32)
    pair_table = draw_pair_table(jax.random.fold_in(jax.random.fold_in(arg_keys[5], part), 71), part)
    return {"raw_record": raw_record, "fir_taps": fir_taps, "channel_ids": channel_ids, "offsets": offsets, "pair_table": pair_table}


def forward_table(length):
    sample = jnp.arange(length, dtype=jnp.int32)[:, None]
    bin_index = jnp.arange(length // 2, dtype=jnp.int32)[None, :]
    angles = (sample * bin_index % length).astype(jnp.float32) * (2.0 * math.pi / length)
    return jnp.concatenate([jnp.cos(angles), -jnp.sin(angles)], axis=1).astype(jnp.bfloat16)

def inverse_table(length):
    bin_index = jnp.arange(length // 2, dtype=jnp.int32)[:, None]
    lag_index = jnp.arange(length, dtype=jnp.int32)[None, :]
    shifted = (lag_index + length // 2) % length
    angles = (bin_index * shifted % length).astype(jnp.float32) * (2.0 * math.pi / length)
    weight = jnp.where(bin_index == 0, 1.0, 2.0).astype(jnp.float32) / math.sqrt(length)
    return jnp.concatenate([weight * jnp.cos(angles), -weight * jnp.sin(angles)], axis=0).astype(jnp.bfloat16)

def whiten(spectrum):
    power_all = spectrum[:, :, 0] ** 2 + spectrum[:, :, 1] ** 2
    extent = power_all.shape
    banded = lax.optimization_barrier(jnp.mean(power_all.reshape(extent[0], extent[1], extent[2] // BAND, BAND), axis=-1))
    inverse_rms = jnp.repeat(lax.rsqrt(banded + 1e-06), BAND, axis=-1)
    return (spectrum * inverse_rms[:, :, None, :]).astype(jnp.bfloat16)

def reference(raw_record, fir_taps, channel_ids, offsets, pair_table):
    seg_len = DEC * (NF - 1) + TAPS
    starts = jnp.arange(NSUB, dtype=jnp.int32) // NSUB_DEV * SPAN + offsets

    def cut_window(start_at):
        return lax.dynamic_slice_in_dim(raw_record, start_at, seg_len, 1)
    windows = jax.vmap(cut_window, out_axes=1)(starts).astype(jnp.float32)
    accum = jnp.zeros((CH, NSUB, NF), jnp.float32)
    for tap_index in range(TAPS):
        accum = accum + fir_taps[tap_index] * windows[:, :, tap_index:tap_index + DEC * (NF - 1) + 1:DEC]
    decimated = accum.astype(jnp.bfloat16)
    spectrum = jnp.dot(decimated.reshape(CH * NSUB, NF), forward_table(NF), preferred_element_type=jnp.float32)
    whitened = whiten(spectrum.reshape(CH, NSUB, 2, NF // 2))
    by_channel = jnp.take(whitened, jnp.argsort(channel_ids).astype(jnp.int32), axis=0)
    lag_table = inverse_table(NF)

    def one_slot(slot_entry):
        live_slot = slot_entry[0] >= 0
        first_rows = lax.dynamic_slice_in_dim(by_channel, jnp.maximum(slot_entry[0], 0) * BLK, BLK, 0).astype(jnp.float32)
        second_rows = lax.dynamic_slice_in_dim(by_channel, jnp.maximum(slot_entry[1], 0) * BLK, BLK, 0).astype(jnp.float32)
        real_part = jnp.einsum('awk,bwk->abk', first_rows[:, :, 0], second_rows[:, :, 0]) + jnp.einsum('awk,bwk->abk', first_rows[:, :, 1], second_rows[:, :, 1])
        imag_part = jnp.einsum('awk,bwk->abk', first_rows[:, :, 1], second_rows[:, :, 0]) - jnp.einsum('awk,bwk->abk', first_rows[:, :, 0], second_rows[:, :, 1])
        cross_bins = jnp.stack([real_part, imag_part], axis=2) / NSUB
        cross_bins = jnp.where(live_slot, cross_bins, 0.0).astype(jnp.bfloat16)
        return jnp.dot(cross_bins.reshape(BLK * BLK, NF), lag_table, preferred_element_type=jnp.float32).reshape(BLK, BLK, NF)
    all_lags = lax.map(one_slot, pair_table)
    return jnp.transpose(all_lags, (1, 0, 2, 3))
```

```python
import functools
import math

import jax
import jax.numpy as jnp
import ml_dtypes
import numpy as np
from jax import lax
from jax.experimental import pallas as pl
from jax.experimental.pallas import tpu as pltpu
from jax.sharding import PartitionSpec as P

NF = 2048
TAPS = 64
DEC = 4
BAND = 64
LANES = 128
HALF = LANES // 2
COARSE = NF // LANES

CHUNK_STEP = DEC * LANES // LANES
WINDOW_CHUNKS = CHUNK_STEP * (COARSE - 1) + 6
GRAIN = LANES // DEC


def two_terms(values):
    high = values.astype(ml_dtypes.bfloat16)
    low = (values - high.astype(np.float64)).astype(ml_dtypes.bfloat16)
    return high, low


def forward_constants(rows, windows):
    k1 = np.arange(COARSE)
    fine = np.arange(LANES)
    k2 = np.arange(HALF)
    angle_a = 2 * np.pi * np.outer(k1, np.arange(COARSE)) / COARSE
    count = rows * windows
    blocks = np.zeros((2, rows, windows, COARSE, windows, rows, COARSE))
    for r in range(rows):
        for w in range(windows):
            blocks[0, r, w, :, w, r, :] = np.cos(angle_a)
            blocks[1, r, w, :, w, r, :] = -np.sin(angle_a)
    high, low = two_terms(blocks.reshape(2 * count * COARSE, count * COARSE))
    step_a = np.concatenate([high, low], axis=1)
    angle_t = 2 * np.pi * np.outer(k1, fine) / NF
    twiddle = np.concatenate([np.cos(angle_t), -np.sin(angle_t)], axis=0).astype(np.float32)
    angle_b = 2 * np.pi * np.outer(fine, k2) / LANES
    cos_b, sin_b = np.cos(angle_b), np.sin(angle_b)
    table = np.concatenate(
        [np.concatenate([cos_b, -sin_b], axis=1), np.concatenate([sin_b, cos_b], axis=1)], axis=0
    )
    high, low = two_terms(table)
    step_b = np.concatenate([high, high, low], axis=0)
    band_of = np.tile(k2 * COARSE // BAND, 2)
    same_band = (band_of[:, None] == band_of[None, :]).astype(ml_dtypes.bfloat16)
    return step_a, twiddle, step_b, same_band


def inverse_constants(block_rows):
    k1 = np.arange(COARSE)
    k2 = np.arange(HALF)
    j1 = np.arange(LANES)
    angle_b = 2 * np.pi * np.outer(k2, j1) / LANES
    cos_b, sin_b = np.cos(angle_b), np.sin(angle_b)
    table = np.concatenate(
        [np.concatenate([cos_b, sin_b], axis=1), np.concatenate([-sin_b, cos_b], axis=1)], axis=0
    )
    step_b = np.concatenate(two_terms(table), axis=0)
    sign = np.where(k1 % 2 == 0, 1.0, -1.0)[:, None] / math.sqrt(NF)
    angle_t = 2 * np.pi * np.outer(k1, j1) / NF
    twiddle = np.concatenate([sign * np.cos(angle_t), sign * np.sin(angle_t)], axis=0)
    angle_a = 2 * np.pi * np.outer(np.arange(COARSE), k1) / COARSE
    blocks = np.zeros((COARSE, block_rows, 2, block_rows, COARSE))
    for b in range(block_rows):
        blocks[:, b, 0, b, :] = np.cos(angle_a)
        blocks[:, b, 1, b, :] = -np.sin(angle_a)
    high, low = two_terms(blocks.reshape(COARSE * block_rows, 2 * block_rows * COARSE))
    step_a = np.concatenate([high, high, low], axis=1)
    return step_b, twiddle.astype(np.float32), step_a


def split_terms(values):
    high = values.astype(jnp.bfloat16)
    low = (values - high.astype(jnp.float32)).astype(jnp.bfloat16)
    return high, low


def spectra_kernel(
    offsets_ref, taps_ref, raw_ref, step_a_ref, twiddle_ref, step_b_ref, band_ref, out_ref, chunks, padded
):
    rows = raw_ref.shape[0]
    windows = offsets_ref.shape[0]
    count = rows * windows
    chunk_total = raw_ref.shape[1] // LANES
    padded[...] = jnp.zeros_like(padded)
    padded[0:1, 0:TAPS] = taps_ref[...]
    plain = jnp.broadcast_to(padded[0:1, :], padded.shape)
    sublane = lax.broadcasted_iota(jnp.int32, padded.shape, 0)
    stair = plain
    for i in range(1, 8):
        stair = jnp.where(sublane == i, pltpu.roll(plain, DEC * i, 1), stair)
    stair = jnp.concatenate([stair, jnp.zeros((8, 2 * LANES), jnp.float32)], axis=1)
    empty = jnp.zeros((GRAIN, LANES), jnp.float32)
    parts = []
    for w in range(windows):
        start = offsets_ref[w]
        first = jnp.minimum(start // LANES, chunk_total - WINDOW_CHUNKS)
        shift = start - first * LANES
        slab = raw_ref[:, pl.ds(pl.multiple_of(first * LANES, LANES), WINDOW_CHUNKS * LANES)].astype(
            jnp.float32
        )
        for c in range(WINDOW_CHUNKS):
            chunks[w, rows * c : rows * (c + 1), :] = slab[:, c * LANES : (c + 1) * LANES]
        band = jnp.concatenate(
            [pltpu.roll(stair, shift + 8 * DEC * g, 1) for g in range(GRAIN // 8)], axis=0
        )
        left = []
        filt = []
        for m in range(6):
            pieces = [
                chunks[w, pl.ds(rows * m + r, COARSE, stride=rows * CHUNK_STEP), :] for r in range(rows)
            ]
            left.append(jnp.concatenate(pieces, axis=0).astype(jnp.bfloat16))
            column = [
                band[:, (m - g) * LANES : (m - g + 1) * LANES] if 0 <= m - g < 3 else empty
                for g in range(DEC)
            ]
            filt.append(jnp.concatenate(column, axis=0))
        left = jnp.concatenate(left, axis=1)
        filt = jnp.concatenate(split_terms(jnp.concatenate(filt, axis=1)), axis=0)
        both = lax.dot_general(
            left, filt, (((1,), (1,)), ((), ())), preferred_element_type=jnp.float32
        )
        parts.append((both[:, :LANES] + both[:, LANES:]).astype(jnp.bfloat16))
    decimated = jnp.concatenate(parts, axis=0)
    coarse = jnp.dot(
        step_a_ref[...], jnp.concatenate([decimated, decimated], axis=0), preferred_element_type=jnp.float32
    )
    size = count * COARSE
    real = coarse[:size].reshape(count, COARSE, LANES)
    imag = coarse[size:].reshape(count, COARSE, LANES)
    cos_t = twiddle_ref[:COARSE][None]
    sin_t = twiddle_ref[COARSE:][None]
    turned = jnp.concatenate(
        [
            (real * cos_t - imag * sin_t).reshape(size, LANES),
            (real * sin_t + imag * cos_t).reshape(size, LANES),
        ],
        axis=1,
    )
    high, low = split_terms(turned)
    spectrum = jnp.dot(
        jnp.concatenate([high, low, high], axis=1), step_b_ref[...], preferred_element_type=jnp.float32
    ).reshape(count, COARSE, LANES)
    power = jnp.sum(spectrum * spectrum, axis=1)
    high, low = split_terms(power)
    banded = jnp.dot(high, band_ref[...], preferred_element_type=jnp.float32) + jnp.dot(
        low, band_ref[...], preferred_element_type=jnp.float32
    )
    inverse_rms = lax.rsqrt(banded * (1.0 / BAND) + 1e-06)
    out_ref[...] = (spectrum * inverse_rms[:, None, :]).reshape(size, LANES).astype(jnp.bfloat16)


def correlate_kernel(
    plan, groups_of, ids_ref, table_ref, step_b_ref, twiddle_ref, step_a_ref, *refs
):
    piece_refs = refs[: len(plan)]
    out_ref, gathered, row_of = refs[len(plan) :]
    pairs, sections, subs = groups_of
    a_count, slots, block_rows = out_ref.shape[:3]
    rows_total, windows_total = gathered.shape[:2]
    channels = ids_ref.shape[0]
    rows = rows_total // (pairs * sections)
    windows = windows_total // subs
    tile = rows * windows * COARSE
    my_pair = lax.axis_index("pairs")
    my_section = lax.axis_index("section")
    my_sub = lax.axis_index("sub")

    for c in range(channels):
        row_of[ids_ref[c]] = c

    for ref, blocks in zip(piece_refs, plan):
        for q, (locate, offset) in enumerate(blocks):
            pair, section, sub = locate(my_pair, my_section, my_sub)
            base_row = (pair * sections + section) * rows
            base_window = sub * windows
            for r in range(rows):
                for w in range(windows):
                    at = offset + (r * windows + w) * COARSE
                    gathered[base_row + r, base_window + w] = ref[at : at + COARSE, :]

    lane = lax.broadcasted_iota(jnp.int32, (COARSE, LANES), 1)
    coarse_bin = lax.broadcasted_iota(jnp.int32, (COARSE, LANES), 0)
    in_left = lane < HALF
    is_zero_bin = (coarse_bin == 0) & (lane % HALF == 0)
    weight = jnp.where(is_zero_bin, 1.0, 2.0) * (1.0 / windows_total)
    cos_t = twiddle_ref[:COARSE][None]
    sin_t = twiddle_ref[COARSE:][None]
    size = block_rows * COARSE
    first_a = (my_section * subs + my_sub) * a_count

    def one_slot(s, carry):
        first_block = table_ref[my_pair * slots + s, 0]
        second_block = table_ref[my_pair * slots + s, 1]
        live = jnp.where(first_block >= 0, 1.0, 0.0)
        scale = weight * live
        first_block = jnp.maximum(first_block, 0)
        second_block = jnp.maximum(second_block, 0)
        ones, turns = [], []
        for a in range(a_count):
            row = row_of[first_block * block_rows + first_a + a]
            one = [gathered[row, w].astype(jnp.float32) for w in range(windows_total)]
            ones.append(one)
            turns.append([jnp.where(in_left, 1.0, -1.0) * pltpu.roll(v, HALF, 1) for v in one])
        crosses = [[] for _ in range(a_count)]
        for b in range(block_rows):
            row = row_of[second_block * block_rows + b]
            other = [gathered[row, w].astype(jnp.float32) for w in range(windows_total)]
            for a in range(a_count):
                even = ones[a][0] * other[0]
                odd = turns[a][0] * other[0]
                for w in range(1, windows_total):
                    even = even + ones[a][w] * other[w]
                    odd = odd + turns[a][w] * other[w]
                cross = jnp.where(in_left, even, odd) + pltpu.roll(jnp.where(in_left, odd, even), HALF, 1)
                crosses[a].append((cross * scale).astype(jnp.bfloat16))
        cross = jnp.concatenate([c for per_a in crosses for c in per_a], axis=0)
        fine = jnp.dot(
            jnp.concatenate([cross, cross], axis=1), step_b_ref[...], preferred_element_type=jnp.float32
        ).reshape(a_count * block_rows, COARSE, 2 * LANES)
        real, imag = fine[:, :, :LANES], fine[:, :, LANES:]
        turned_real = (real * cos_t - imag * sin_t).reshape(a_count, size, LANES)
        turned_imag = (real * sin_t + imag * cos_t).reshape(a_count, size, LANES)
        turned = jnp.concatenate(
            [
                jnp.concatenate([turned_real[a] for a in range(a_count)], axis=1),
                jnp.concatenate([turned_imag[a] for a in range(a_count)], axis=1),
            ],
            axis=0,
        )
        high, low = split_terms(turned)
        lags = jnp.dot(
            step_a_ref[...], jnp.concatenate([high, low, high], axis=0), preferred_element_type=jnp.float32
        )
        for a in range(a_count):
            for j2 in range(COARSE):
                out_ref[a, s, :, j2 * LANES : (j2 + 1) * LANES] = lags[
                    j2 * block_rows : (j2 + 1) * block_rows, a * LANES : (a + 1) * LANES
                ]
        return carry

    if slots <= 4:
        for s in range(slots):
            one_slot(s, 0)
    else:
        lax.fori_loop(0, slots, one_slot, 0)


def exchange(mine, sizes):
    pairs, sections, subs = sizes
    block = mine.shape[0]
    axes = ("pairs", "section", "sub")
    if (pairs, sections, subs) != (4, 2, 2):
        everything = lax.all_gather(mine, axes, axis=0, tiled=True)
        blocks = []
        for z in range(pairs):
            for s in range(sections):
                for x in range(subs):
                    blocks.append(
                        ((lambda p, q, u, z=z, s=s, x=x: (z, s, x)), ((z * sections + s) * subs + x) * block)
                    )
        return [everything], [blocks]

    def chips(value, *deltas):
        moves = []
        for z in range(pairs):
            for x in range(subs):
                for s in range(sections):
                    dz, dx = deltas[s % len(deltas)]
                    moves.append((((z * sections + s) * subs + x), ((z ^ dz) * sections + s) * subs + (x ^ dx)))
        return lax.ppermute(value, axes, moves)

    def cores(value):
        return lax.ppermute(value, "section", [(0, 1), (1, 0)])

    far = (3, 1)
    rounds = (((0, 1), (1, 0)), ((1, 1), (2, 0)), ((2, 1), (3, 0)))
    pieces = [mine]
    plan = [[((lambda p, q, u: (p, q, u)), 0)]]
    direct = chips(mine, far)
    other = cores(mine)
    pieces.append(other)
    plan.append([((lambda p, q, u: (p, 1 - q, u)), 0)])
    pieces.append(direct)
    plan.append([((lambda p, q, u: (p ^ far[0], q, u ^ far[1])), 0)])
    pieces.append(cores(direct))
    plan.append([((lambda p, q, u: (p ^ far[0], 1 - q, u ^ far[1])), 0)])
    both = jnp.concatenate([mine, other], axis=0)
    for d0, d1 in rounds:
        arrived = chips(both, d0, d1)

        def here(p, q, u, d0=d0, d1=d1):
            return (p ^ jnp.where(q == 0, d0[0], d1[0]), q, u ^ jnp.where(q == 0, d0[1], d1[1]))

        def here_flip(p, q, u, here=here):
            z, s, x = here(p, q, u)
            return z, 1 - s, x

        def there(p, q, u, here=here):
            return here(p, 1 - q, u)

        def there_flip(p, q, u, there=there):
            z, s, x = there(p, q, u)
            return z, 1 - s, x

        pieces.append(arrived)
        plan.append([(here, 0), (here_flip, block)])
        pieces.append(cores(arrived))
        plan.append([(there, 0), (there_flip, block)])
    return pieces, plan


def body(raw_record, fir_taps, channel_ids, offsets, pair_table):
    rows = raw_record.shape[0]
    windows = offsets.shape[0]
    sizes = tuple(lax.axis_size(name) for name in ("pairs", "section", "sub"))
    pairs, sections, subs = sizes
    block_rows = rows * sections
    slots = pair_table.shape[0] // pairs
    a_count = block_rows // (sections * subs)
    vmem = pl.BlockSpec(memory_space=pltpu.VMEM)
    smem = pl.BlockSpec(memory_space=pltpu.SMEM)

    consts = [jnp.asarray(c) for c in forward_constants(rows, windows)]
    whitened = pl.pallas_call(
        spectra_kernel,
        name="spectra",
        out_shape=jax.ShapeDtypeStruct((rows * windows * COARSE, LANES), jnp.bfloat16),
        in_specs=[smem] + [vmem] * 6,
        out_specs=vmem,
        scratch_shapes=[
            pltpu.VMEM((windows, rows * WINDOW_CHUNKS, LANES), jnp.float32),
            pltpu.VMEM((8, LANES), jnp.float32),
        ],
        compiler_params=pltpu.CompilerParams(vmem_limit_bytes=32 * 1024 * 1024),
    )(offsets, fir_taps.reshape(1, TAPS), raw_record, *consts)

    pieces, plan = exchange(whitened, sizes)

    consts = [jnp.asarray(c) for c in inverse_constants(block_rows)]
    return pl.pallas_call(
        functools.partial(correlate_kernel, plan, sizes),
        name="correlate",
        out_shape=jax.ShapeDtypeStruct((a_count, slots, block_rows, NF), jnp.float32),
        in_specs=[smem, smem] + [vmem] * (3 + len(pieces)),
        out_specs=vmem,
        scratch_shapes=[
            pltpu.VMEM((rows * pairs * sections, windows * subs, COARSE, LANES), jnp.bfloat16),
            pltpu.SMEM((channel_ids.shape[0],), jnp.int32),
        ],
        compiler_params=pltpu.CompilerParams(vmem_limit_bytes=32 * 1024 * 1024),
    )(channel_ids, pair_table, *consts, *pieces)


def solution(mesh):
    return jax.shard_map(
        body,
        mesh=mesh,
        in_specs=(
            P(("groups", "pairs", "section"), "sub"),
            P(),
            P("groups"),
            P(("groups", "sub")),
            P("groups", None),
        ),
        out_specs=P(("section", "sub"), ("groups", "pairs"), None, None),
        check_vma=False,
    )
```

```python
import functools
import math

import jax
import jax.numpy as jnp
import ml_dtypes
import numpy as np
from jax import lax
from jax.experimental import pallas as pl
from jax.experimental.pallas import tpu as pltpu
from jax.sharding import PartitionSpec as P

NF = 2048
TAPS = 64
DEC = 4
BAND = 64
LANES = 128
HALF = LANES // 2
COARSE = NF // LANES

CHUNK_STEP = DEC * LANES // LANES
WINDOW_CHUNKS = CHUNK_STEP * (COARSE - 1) + 6
GRAIN = LANES // DEC


def two_terms(values):
    high = values.astype(ml_dtypes.bfloat16)
    low = (values - high.astype(np.float64)).astype(ml_dtypes.bfloat16)
    return high, low


def forward_constants(rows, windows):
    k1 = np.arange(COARSE)
    fine = np.arange(LANES)
    k2 = np.arange(HALF)
    angle_a = 2 * np.pi * np.outer(k1, np.arange(COARSE)) / COARSE
    count = rows * windows
    blocks = np.zeros((2, rows, windows, COARSE, windows, rows, COARSE))
    for r in range(rows):
        for w in range(windows):
            blocks[0, r, w, :, w, r, :] = np.cos(angle_a)
            blocks[1, r, w, :, w, r, :] = -np.sin(angle_a)
    high, low = two_terms(blocks.reshape(2 * count * COARSE, count * COARSE))
    step_a = np.concatenate([high, low], axis=1)
    angle_t = 2 * np.pi * np.outer(k1, fine) / NF
    twiddle = np.concatenate([np.cos(angle_t), -np.sin(angle_t)], axis=0).astype(np.float32)
    angle_b = 2 * np.pi * np.outer(fine, k2) / LANES
    cos_b, sin_b = np.cos(angle_b), np.sin(angle_b)
    table = np.concatenate(
        [np.concatenate([cos_b, -sin_b], axis=1), np.concatenate([sin_b, cos_b], axis=1)], axis=0
    )
    high, low = two_terms(table)
    step_b = np.concatenate([high, high, low], axis=0)
    band_of = np.tile(k2 * COARSE // BAND, 2)
    same_band = (band_of[:, None] == band_of[None, :]).astype(ml_dtypes.bfloat16)
    return step_a, twiddle, step_b, same_band


def inverse_constants(block_rows):
    k1 = np.arange(COARSE)
    k2 = np.arange(HALF)
    j1 = np.arange(LANES)
    angle_b = 2 * np.pi * np.outer(k2, j1) / LANES
    cos_b, sin_b = np.cos(angle_b), np.sin(angle_b)
    table = np.concatenate(
        [np.concatenate([cos_b, sin_b], axis=1), np.concatenate([-sin_b, cos_b], axis=1)], axis=0
    )
    step_b = np.concatenate(two_terms(table), axis=0)
    sign = np.where(k1 % 2 == 0, 1.0, -1.0)[:, None] / math.sqrt(NF)
    angle_t = 2 * np.pi * np.outer(k1, j1) / NF
    twiddle = np.concatenate([sign * np.cos(angle_t), sign * np.sin(angle_t)], axis=0)
    angle_a = 2 * np.pi * np.outer(np.arange(COARSE), k1) / COARSE
    blocks = np.zeros((COARSE, block_rows, 2, block_rows, COARSE))
    for b in range(block_rows):
        blocks[:, b, 0, b, :] = np.cos(angle_a)
        blocks[:, b, 1, b, :] = -np.sin(angle_a)
    high, low = two_terms(blocks.reshape(COARSE * block_rows, 2 * block_rows * COARSE))
    step_a = np.concatenate([high, high, low], axis=1)
    return step_b, twiddle.astype(np.float32), step_a


def split_terms(values):
    high = values.astype(jnp.bfloat16)
    low = (values - high.astype(jnp.float32)).astype(jnp.bfloat16)
    return high, low


def spectra_kernel(
    offsets_hbm,
    taps_hbm,
    raw_hbm,
    step_a_hbm,
    twiddle_hbm,
    step_b_hbm,
    band_hbm,
    out_ref,
    offsets_ref,
    taps_ref,
    raw_ref,
    step_a_ref,
    twiddle_ref,
    step_b_ref,
    band_ref,
    chunks,
    padded,
    arrived,
):
    sources = (offsets_hbm, taps_hbm, raw_hbm, step_a_hbm, twiddle_hbm, step_b_hbm, band_hbm)
    places = (offsets_ref, taps_ref, raw_ref, step_a_ref, twiddle_ref, step_b_ref, band_ref)
    copies = [
        pltpu.make_async_copy(source, place, arrived.at[q])
        for q, (source, place) in enumerate(zip(sources, places))
    ]
    for copy in copies:
        copy.start()
    rows = raw_ref.shape[0]
    windows = offsets_ref.shape[0]
    count = rows * windows
    chunk_total = raw_ref.shape[1] // LANES
    padded[...] = jnp.zeros_like(padded)
    copies[1].wait()
    padded[0:1, 0:TAPS] = taps_ref[...]
    plain = jnp.broadcast_to(padded[0:1, :], padded.shape)
    sublane = lax.broadcasted_iota(jnp.int32, padded.shape, 0)
    stair = plain
    for i in range(1, 8):
        stair = jnp.where(sublane == i, pltpu.roll(plain, DEC * i, 1), stair)
    stair = jnp.concatenate([stair, jnp.zeros((8, 2 * LANES), jnp.float32)], axis=1)
    empty = jnp.zeros((GRAIN, LANES), jnp.float32)
    parts = []
    copies[0].wait()
    copies[2].wait()
    for w in range(windows):
        start = offsets_ref[w]
        first = jnp.minimum(start // LANES, chunk_total - WINDOW_CHUNKS)
        shift = start - first * LANES
        slab = raw_ref[:, pl.ds(pl.multiple_of(first * LANES, LANES), WINDOW_CHUNKS * LANES)].astype(
            jnp.float32
        )
        for c in range(WINDOW_CHUNKS):
            chunks[w, rows * c : rows * (c + 1), :] = slab[:, c * LANES : (c + 1) * LANES]
        band = jnp.concatenate(
            [pltpu.roll(stair, shift + 8 * DEC * g, 1) for g in range(GRAIN // 8)], axis=0
        )
        left = []
        filt = []
        for m in range(6):
            pieces = [
                chunks[w, pl.ds(rows * m + r, COARSE, stride=rows * CHUNK_STEP), :] for r in range(rows)
            ]
            left.append(jnp.concatenate(pieces, axis=0).astype(jnp.bfloat16))
            column = [
                band[:, (m - g) * LANES : (m - g + 1) * LANES] if 0 <= m - g < 3 else empty
                for g in range(DEC)
            ]
            filt.append(jnp.concatenate(column, axis=0))
        left = jnp.concatenate(left, axis=1)
        filt = jnp.concatenate(split_terms(jnp.concatenate(filt, axis=1)), axis=0)
        both = lax.dot_general(
            left, filt, (((1,), (1,)), ((), ())), preferred_element_type=jnp.float32
        )
        parts.append((both[:, :LANES] + both[:, LANES:]).astype(jnp.bfloat16))
    decimated = jnp.concatenate(parts, axis=0)
    copies[3].wait()
    coarse = jnp.dot(
        step_a_ref[...], jnp.concatenate([decimated, decimated], axis=0), preferred_element_type=jnp.float32
    )
    size = count * COARSE
    real = coarse[:size].reshape(count, COARSE, LANES)
    imag = coarse[size:].reshape(count, COARSE, LANES)
    copies[4].wait()
    cos_t = twiddle_ref[:COARSE][None]
    sin_t = twiddle_ref[COARSE:][None]
    turned = jnp.concatenate(
        [
            (real * cos_t - imag * sin_t).reshape(size, LANES),
            (real * sin_t + imag * cos_t).reshape(size, LANES),
        ],
        axis=1,
    )
    high, low = split_terms(turned)
    copies[5].wait()
    spectrum = jnp.dot(
        jnp.concatenate([high, low, high], axis=1), step_b_ref[...], preferred_element_type=jnp.float32
    ).reshape(count, COARSE, LANES)
    power = jnp.sum(spectrum * spectrum, axis=1)
    high, low = split_terms(power)
    copies[6].wait()
    banded = jnp.dot(high, band_ref[...], preferred_element_type=jnp.float32) + jnp.dot(
        low, band_ref[...], preferred_element_type=jnp.float32
    )
    inverse_rms = lax.rsqrt(banded * (1.0 / BAND) + 1e-06)
    out_ref[...] = (spectrum * inverse_rms[:, None, :]).reshape(size, LANES).astype(jnp.bfloat16)


def correlate_kernel(
    plan, groups_of, ids_ref, table_ref, step_b_ref, twiddle_ref, step_a_ref, *refs
):
    piece_refs = refs[: len(plan)]
    out_ref, gathered, row_of = refs[len(plan) :]
    pairs, sections, subs = groups_of
    a_count, slots, block_rows = out_ref.shape[:3]
    rows_total, windows_total = gathered.shape[:2]
    channels = ids_ref.shape[0]
    rows = rows_total // (pairs * sections)
    windows = windows_total // subs
    tile = rows * windows * COARSE
    my_pair = lax.axis_index("pairs")
    my_section = lax.axis_index("section")
    my_sub = lax.axis_index("sub")

    for c in range(channels):
        row_of[ids_ref[c]] = c

    for ref, blocks in zip(piece_refs, plan):
        for q, (locate, offset) in enumerate(blocks):
            pair, section, sub = locate(my_pair, my_section, my_sub)
            base_row = (pair * sections + section) * rows
            base_window = sub * windows
            for r in range(rows):
                for w in range(windows):
                    at = offset + (r * windows + w) * COARSE
                    gathered[base_row + r, base_window + w] = ref[at : at + COARSE, :]

    lane = lax.broadcasted_iota(jnp.int32, (COARSE, LANES), 1)
    coarse_bin = lax.broadcasted_iota(jnp.int32, (COARSE, LANES), 0)
    in_left = lane < HALF
    is_zero_bin = (coarse_bin == 0) & (lane % HALF == 0)
    weight = jnp.where(is_zero_bin, 1.0, 2.0) * (1.0 / windows_total)
    cos_t = twiddle_ref[:COARSE][None]
    sin_t = twiddle_ref[COARSE:][None]
    size = block_rows * COARSE
    first_a = (my_section * subs + my_sub) * a_count

    def one_slot(s, carry):
        first_block = table_ref[my_pair * slots + s, 0]
        second_block = table_ref[my_pair * slots + s, 1]
        live = jnp.where(first_block >= 0, 1.0, 0.0)
        scale = weight * live
        first_block = jnp.maximum(first_block, 0)
        second_block = jnp.maximum(second_block, 0)
        ones, turns = [], []
        for a in range(a_count):
            row = row_of[first_block * block_rows + first_a + a]
            one = [gathered[row, w].astype(jnp.float32) for w in range(windows_total)]
            ones.append(one)
            turns.append([jnp.where(in_left, 1.0, -1.0) * pltpu.roll(v, HALF, 1) for v in one])
        crosses = [[] for _ in range(a_count)]
        for b in range(block_rows):
            row = row_of[second_block * block_rows + b]
            other = [gathered[row, w].astype(jnp.float32) for w in range(windows_total)]
            for a in range(a_count):
                even = ones[a][0] * other[0]
                odd = turns[a][0] * other[0]
                for w in range(1, windows_total):
                    even = even + ones[a][w] * other[w]
                    odd = odd + turns[a][w] * other[w]
                cross = jnp.where(in_left, even, odd) + pltpu.roll(jnp.where(in_left, odd, even), HALF, 1)
                crosses[a].append((cross * scale).astype(jnp.bfloat16))
        cross = jnp.concatenate([c for per_a in crosses for c in per_a], axis=0)
        fine = jnp.dot(
            jnp.concatenate([cross, cross], axis=1), step_b_ref[...], preferred_element_type=jnp.float32
        ).reshape(a_count * block_rows, COARSE, 2 * LANES)
        real, imag = fine[:, :, :LANES], fine[:, :, LANES:]
        turned_real = (real * cos_t - imag * sin_t).reshape(a_count, size, LANES)
        turned_imag = (real * sin_t + imag * cos_t).reshape(a_count, size, LANES)
        turned = jnp.concatenate(
            [
                jnp.concatenate([turned_real[a] for a in range(a_count)], axis=1),
                jnp.concatenate([turned_imag[a] for a in range(a_count)], axis=1),
            ],
            axis=0,
        )
        high, low = split_terms(turned)
        lags = jnp.dot(
            step_a_ref[...], jnp.concatenate([high, low, high], axis=0), preferred_element_type=jnp.float32
        )
        for a in range(a_count):
            for j2 in range(COARSE):
                out_ref[a, s, :, j2 * LANES : (j2 + 1) * LANES] = lags[
                    j2 * block_rows : (j2 + 1) * block_rows, a * LANES : (a + 1) * LANES
                ]
        return carry

    if slots <= 4:
        for s in range(slots):
            one_slot(s, 0)
    else:
        lax.fori_loop(0, slots, one_slot, 0)


def exchange(mine, sizes):
    pairs, sections, subs = sizes
    block = mine.shape[0]
    axes = ("pairs", "section", "sub")
    if (pairs, sections, subs) != (4, 2, 2):
        everything = lax.all_gather(mine, axes, axis=0, tiled=True)
        blocks = []
        for z in range(pairs):
            for s in range(sections):
                for x in range(subs):
                    blocks.append(
                        ((lambda p, q, u, z=z, s=s, x=x: (z, s, x)), ((z * sections + s) * subs + x) * block)
                    )
        return [everything], [blocks]

    def chips(value, *deltas):
        moves = []
        for z in range(pairs):
            for x in range(subs):
                for s in range(sections):
                    dz, dx = deltas[s % len(deltas)]
                    moves.append((((z * sections + s) * subs + x), ((z ^ dz) * sections + s) * subs + (x ^ dx)))
        return lax.ppermute(value, axes, moves)

    def cores(value):
        return lax.ppermute(value, "section", [(0, 1), (1, 0)])

    far = (3, 1)
    rounds = (((0, 1), (1, 0)), ((1, 1), (2, 0)), ((2, 1), (3, 0)))
    pieces = [mine]
    plan = [[((lambda p, q, u: (p, q, u)), 0)]]
    direct = chips(mine, far)
    other = cores(mine)
    pieces.append(other)
    plan.append([((lambda p, q, u: (p, 1 - q, u)), 0)])
    pieces.append(direct)
    plan.append([((lambda p, q, u: (p ^ far[0], q, u ^ far[1])), 0)])
    pieces.append(cores(direct))
    plan.append([((lambda p, q, u: (p ^ far[0], 1 - q, u ^ far[1])), 0)])
    both = jnp.concatenate([mine, other], axis=0)
    for d0, d1 in rounds:
        arrived = chips(both, d0, d1)

        def here(p, q, u, d0=d0, d1=d1):
            return (p ^ jnp.where(q == 0, d0[0], d1[0]), q, u ^ jnp.where(q == 0, d0[1], d1[1]))

        def here_flip(p, q, u, here=here):
            z, s, x = here(p, q, u)
            return z, 1 - s, x

        def there(p, q, u, here=here):
            return here(p, 1 - q, u)

        def there_flip(p, q, u, there=there):
            z, s, x = there(p, q, u)
            return z, 1 - s, x

        pieces.append(arrived)
        plan.append([(here, 0), (here_flip, block)])
        pieces.append(cores(arrived))
        plan.append([(there, 0), (there_flip, block)])
    return pieces, plan


def body(raw_record, fir_taps, channel_ids, offsets, pair_table):
    rows = raw_record.shape[0]
    windows = offsets.shape[0]
    sizes = tuple(lax.axis_size(name) for name in ("pairs", "section", "sub"))
    pairs, sections, subs = sizes
    block_rows = rows * sections
    slots = pair_table.shape[0] // pairs
    a_count = block_rows // (sections * subs)
    vmem = pl.BlockSpec(memory_space=pltpu.VMEM)
    smem = pl.BlockSpec(memory_space=pltpu.SMEM)

    operands = [offsets, fir_taps.reshape(1, TAPS), raw_record]
    operands += [jnp.asarray(c) for c in forward_constants(rows, windows)]
    operands = [pltpu.with_memory_space_constraint(operand, pltpu.HBM) for operand in operands]
    whitened = pl.pallas_call(
        spectra_kernel,
        name="spectra",
        out_shape=pltpu.VMEM((rows * windows * COARSE, LANES), jnp.bfloat16),
        in_specs=[pl.BlockSpec(memory_space=pltpu.HBM)] * len(operands),
        out_specs=vmem,
        scratch_shapes=[pltpu.SMEM(offsets.shape, offsets.dtype)]
        + [pltpu.VMEM(operand.shape, operand.dtype) for operand in operands[1:]]
        + [
            pltpu.VMEM((windows, rows * WINDOW_CHUNKS, LANES), jnp.float32),
            pltpu.VMEM((8, LANES), jnp.float32),
            pltpu.SemaphoreType.DMA((len(operands),)),
        ],
        compiler_params=pltpu.CompilerParams(vmem_limit_bytes=32 * 1024 * 1024),
    )(*operands)

    pieces, plan = exchange(whitened, sizes)

    consts = [jnp.asarray(c) for c in inverse_constants(block_rows)]
    return pl.pallas_call(
        functools.partial(correlate_kernel, plan, sizes),
        name="correlate",
        out_shape=jax.ShapeDtypeStruct((a_count, slots, block_rows, NF), jnp.float32),
        in_specs=[smem, smem] + [vmem] * (3 + len(pieces)),
        out_specs=vmem,
        scratch_shapes=[
            pltpu.VMEM((rows * pairs * sections, windows * subs, COARSE, LANES), jnp.bfloat16),
            pltpu.SMEM((channel_ids.shape[0],), jnp.int32),
        ],
        compiler_params=pltpu.CompilerParams(vmem_limit_bytes=32 * 1024 * 1024),
    )(channel_ids, pair_table, *consts, *pieces)


def solution(mesh):
    return jax.shard_map(
        body,
        mesh=mesh,
        in_specs=(
            P(("groups", "pairs", "section"), "sub"),
            P(),
            P("groups"),
            P(("groups", "sub")),
            P("groups", None),
        ),
        out_specs=P(("section", "sub"), ("groups", "pairs"), None, None),
        check_vma=False,
    )
```

```python
import functools
import math

import jax
import jax.numpy as jnp
import ml_dtypes
import numpy as np
from jax import lax
from jax.experimental import pallas as pl
from jax.experimental.pallas import tpu as pltpu
from jax.sharding import PartitionSpec as P

NF = 2048
TAPS = 64
DEC = 4
BAND = 64
LANES = 128
HALF = LANES // 2
COARSE = NF // LANES

CHUNK_STEP = DEC * LANES // LANES
WINDOW_CHUNKS = CHUNK_STEP * (COARSE - 1) + 6
STEPS = (((1, 0), (1, 0), 'own'), ((2, 0), (2, 1), 'both'), ((3, 0), (3, 1), 'both'), ((0, 1), (1, 1), 'both'))
ORDER = (3, 2, 1, 0)
GRAIN = LANES // DEC


def two_terms(values):
    high = values.astype(ml_dtypes.bfloat16)
    low = (values - high.astype(np.float64)).astype(ml_dtypes.bfloat16)
    return high, low


def forward_constants(rows, windows):
    k1 = np.arange(COARSE)
    fine = np.arange(LANES)
    k2 = np.arange(HALF)
    angle_a = 2 * np.pi * np.outer(k1, np.arange(COARSE)) / COARSE
    count = rows * windows
    blocks = np.zeros((2, rows, windows, COARSE, windows, rows, COARSE))
    for r in range(rows):
        for w in range(windows):
            blocks[0, r, w, :, w, r, :] = np.cos(angle_a)
            blocks[1, r, w, :, w, r, :] = -np.sin(angle_a)
    high, low = two_terms(blocks.reshape(2 * count * COARSE, count * COARSE))
    step_a = np.concatenate([high, low], axis=1)
    angle_t = 2 * np.pi * np.outer(k1, fine) / NF
    twiddle = np.concatenate([np.cos(angle_t), -np.sin(angle_t)], axis=0).astype(np.float32)
    angle_b = 2 * np.pi * np.outer(fine, k2) / LANES
    cos_b, sin_b = np.cos(angle_b), np.sin(angle_b)
    table = np.concatenate(
        [np.concatenate([cos_b, -sin_b], axis=1), np.concatenate([sin_b, cos_b], axis=1)], axis=0
    )
    high, low = two_terms(table)
    step_b = np.concatenate([high, high, low], axis=0)
    band_of = np.tile(k2 * COARSE // BAND, 2)
    same_band = (band_of[:, None] == band_of[None, :]).astype(ml_dtypes.bfloat16)
    return step_a, twiddle, step_b, same_band


def inverse_constants(block_rows):
    k1 = np.arange(COARSE)
    k2 = np.arange(HALF)
    j1 = np.arange(LANES)
    angle_b = 2 * np.pi * np.outer(k2, j1) / LANES
    cos_b, sin_b = np.cos(angle_b), np.sin(angle_b)
    table = np.concatenate(
        [np.concatenate([cos_b, sin_b], axis=1), np.concatenate([-sin_b, cos_b], axis=1)], axis=0
    )
    step_b = np.concatenate(two_terms(table), axis=0)
    sign = np.where(k1 % 2 == 0, 1.0, -1.0)[:, None] / math.sqrt(NF)
    angle_t = 2 * np.pi * np.outer(k1, j1) / NF
    twiddle = np.concatenate([sign * np.cos(angle_t), sign * np.sin(angle_t)], axis=0)
    angle_a = 2 * np.pi * np.outer(np.arange(COARSE), k1) / COARSE
    blocks = np.zeros((COARSE, block_rows, 2, block_rows, COARSE))
    for b in range(block_rows):
        blocks[:, b, 0, b, :] = np.cos(angle_a)
        blocks[:, b, 1, b, :] = -np.sin(angle_a)
    high, low = two_terms(blocks.reshape(COARSE * block_rows, 2 * block_rows * COARSE))
    step_a = np.concatenate([high, high, low], axis=1)
    return step_b, twiddle.astype(np.float32), step_a


def split_terms(values):
    high = values.astype(jnp.bfloat16)
    low = (values - high.astype(jnp.float32)).astype(jnp.bfloat16)
    return high, low


def spectra_kernel(
    offsets_hbm,
    taps_hbm,
    raw_hbm,
    step_a_hbm,
    twiddle_hbm,
    step_b_hbm,
    band_hbm,
    out_ref,
    offsets_ref,
    taps_ref,
    raw_ref,
    step_a_ref,
    twiddle_ref,
    step_b_ref,
    band_ref,
    chunks,
    padded,
    arrived,
):
    sources = (offsets_hbm, taps_hbm, raw_hbm, step_a_hbm, twiddle_hbm, step_b_hbm, band_hbm)
    places = (offsets_ref, taps_ref, raw_ref, step_a_ref, twiddle_ref, step_b_ref, band_ref)
    copies = [
        pltpu.make_async_copy(source, place, arrived.at[q])
        for q, (source, place) in enumerate(zip(sources, places))
    ]
    for copy in copies:
        copy.start()
    rows = raw_ref.shape[0]
    windows = offsets_ref.shape[0]
    count = rows * windows
    chunk_total = raw_ref.shape[1] // LANES
    padded[...] = jnp.zeros_like(padded)
    copies[1].wait()
    padded[0:1, 0:TAPS] = taps_ref[...]
    plain = jnp.broadcast_to(padded[0:1, :], padded.shape)
    sublane = lax.broadcasted_iota(jnp.int32, padded.shape, 0)
    stair = plain
    for i in range(1, 8):
        stair = jnp.where(sublane == i, pltpu.roll(plain, DEC * i, 1), stair)
    stair = jnp.concatenate([stair, jnp.zeros((8, 2 * LANES), jnp.float32)], axis=1)
    empty = jnp.zeros((GRAIN, LANES), jnp.float32)
    parts = []
    copies[0].wait()
    copies[2].wait()
    for w in range(windows):
        start = offsets_ref[w]
        first = jnp.minimum(start // LANES, chunk_total - WINDOW_CHUNKS)
        shift = start - first * LANES
        slab = raw_ref[:, pl.ds(pl.multiple_of(first * LANES, LANES), WINDOW_CHUNKS * LANES)].astype(
            jnp.float32
        )
        for c in range(WINDOW_CHUNKS):
            chunks[w, rows * c : rows * (c + 1), :] = slab[:, c * LANES : (c + 1) * LANES]
        band = jnp.concatenate(
            [pltpu.roll(stair, shift + 8 * DEC * g, 1) for g in range(GRAIN // 8)], axis=0
        )
        left = []
        filt = []
        for m in range(6):
            pieces = [
                chunks[w, pl.ds(rows * m + r, COARSE, stride=rows * CHUNK_STEP), :] for r in range(rows)
            ]
            left.append(jnp.concatenate(pieces, axis=0).astype(jnp.bfloat16))
            column = [
                band[:, (m - g) * LANES : (m - g + 1) * LANES] if 0 <= m - g < 3 else empty
                for g in range(DEC)
            ]
            filt.append(jnp.concatenate(column, axis=0))
        left = jnp.concatenate(left, axis=1)
        filt = jnp.concatenate(split_terms(jnp.concatenate(filt, axis=1)), axis=0)
        both = lax.dot_general(
            left, filt, (((1,), (1,)), ((), ())), preferred_element_type=jnp.float32
        )
        parts.append((both[:, :LANES] + both[:, LANES:]).astype(jnp.bfloat16))
    decimated = jnp.concatenate(parts, axis=0)
    copies[3].wait()
    coarse = jnp.dot(
        step_a_ref[...], jnp.concatenate([decimated, decimated], axis=0), preferred_element_type=jnp.float32
    )
    size = count * COARSE
    real = coarse[:size].reshape(count, COARSE, LANES)
    imag = coarse[size:].reshape(count, COARSE, LANES)
    copies[4].wait()
    cos_t = twiddle_ref[:COARSE][None]
    sin_t = twiddle_ref[COARSE:][None]
    turned = jnp.concatenate(
        [
            (real * cos_t - imag * sin_t).reshape(size, LANES),
            (real * sin_t + imag * cos_t).reshape(size, LANES),
        ],
        axis=1,
    )
    high, low = split_terms(turned)
    copies[5].wait()
    spectrum = jnp.dot(
        jnp.concatenate([high, low, high], axis=1), step_b_ref[...], preferred_element_type=jnp.float32
    ).reshape(count, COARSE, LANES)
    power = jnp.sum(spectrum * spectrum, axis=1)
    high, low = split_terms(power)
    copies[6].wait()
    banded = jnp.dot(high, band_ref[...], preferred_element_type=jnp.float32) + jnp.dot(
        low, band_ref[...], preferred_element_type=jnp.float32
    )
    inverse_rms = lax.rsqrt(banded * (1.0 / BAND) + 1e-06)
    out_ref[...] = (spectrum * inverse_rms[:, None, :]).reshape(size, LANES).astype(jnp.bfloat16)


def correlate_kernel(
    plan, groups_of, ids_ref, table_ref, step_b_ref, twiddle_ref, step_a_ref, *refs
):
    piece_refs = refs[: len(plan)]
    out_ref, gathered, row_of = refs[len(plan) :]
    pairs, sections, subs = groups_of
    a_count, slots, block_rows = out_ref.shape[:3]
    rows_total, windows_total = gathered.shape[:2]
    channels = ids_ref.shape[0]
    rows = rows_total // (pairs * sections)
    windows = windows_total // subs
    tile = rows * windows * COARSE
    my_pair = lax.axis_index("pairs")
    my_section = lax.axis_index("section")
    my_sub = lax.axis_index("sub")

    for c in range(channels):
        row_of[ids_ref[c]] = c

    for ref, blocks in zip(piece_refs, plan):
        for q, (locate, offset) in enumerate(blocks):
            pair, section, sub = locate(my_pair, my_section, my_sub)
            base_row = (pair * sections + section) * rows
            base_window = sub * windows
            for r in range(rows):
                for w in range(windows):
                    at = offset + (r * windows + w) * COARSE
                    gathered[base_row + r, base_window + w] = ref[at : at + COARSE, :]

    lane = lax.broadcasted_iota(jnp.int32, (COARSE, LANES), 1)
    coarse_bin = lax.broadcasted_iota(jnp.int32, (COARSE, LANES), 0)
    in_left = lane < HALF
    is_zero_bin = (coarse_bin == 0) & (lane % HALF == 0)
    weight = jnp.where(is_zero_bin, 1.0, 2.0) * (1.0 / windows_total)
    cos_t = twiddle_ref[:COARSE][None]
    sin_t = twiddle_ref[COARSE:][None]
    size = block_rows * COARSE
    first_a = (my_section * subs + my_sub) * a_count

    def one_slot(s, carry):
        first_block = table_ref[my_pair * slots + s, 0]
        second_block = table_ref[my_pair * slots + s, 1]
        live = jnp.where(first_block >= 0, 1.0, 0.0)
        scale = weight * live
        first_block = jnp.maximum(first_block, 0)
        second_block = jnp.maximum(second_block, 0)
        ones, turns = [], []
        for a in range(a_count):
            row = row_of[first_block * block_rows + first_a + a]
            one = [gathered[row, w].astype(jnp.float32) for w in range(windows_total)]
            ones.append(one)
            turns.append([jnp.where(in_left, 1.0, -1.0) * pltpu.roll(v, HALF, 1) for v in one])
        crosses = [[] for _ in range(a_count)]
        for b in range(block_rows):
            row = row_of[second_block * block_rows + b]
            other = [gathered[row, w].astype(jnp.float32) for w in range(windows_total)]
            for a in range(a_count):
                even = ones[a][0] * other[0]
                odd = turns[a][0] * other[0]
                for w in range(1, windows_total):
                    even = even + ones[a][w] * other[w]
                    odd = odd + turns[a][w] * other[w]
                cross = jnp.where(in_left, even, odd) + pltpu.roll(jnp.where(in_left, odd, even), HALF, 1)
                crosses[a].append((cross * scale).astype(jnp.bfloat16))
        cross = jnp.concatenate([c for per_a in crosses for c in per_a], axis=0)
        fine = jnp.dot(
            jnp.concatenate([cross, cross], axis=1), step_b_ref[...], preferred_element_type=jnp.float32
        ).reshape(a_count * block_rows, COARSE, 2 * LANES)
        real, imag = fine[:, :, :LANES], fine[:, :, LANES:]
        turned_real = (real * cos_t - imag * sin_t).reshape(a_count, size, LANES)
        turned_imag = (real * sin_t + imag * cos_t).reshape(a_count, size, LANES)
        turned = jnp.concatenate(
            [
                jnp.concatenate([turned_real[a] for a in range(a_count)], axis=1),
                jnp.concatenate([turned_imag[a] for a in range(a_count)], axis=1),
            ],
            axis=0,
        )
        high, low = split_terms(turned)
        lags = jnp.dot(
            step_a_ref[...], jnp.concatenate([high, low, high], axis=0), preferred_element_type=jnp.float32
        )
        for a in range(a_count):
            for j2 in range(COARSE):
                out_ref[a, s, :, j2 * LANES : (j2 + 1) * LANES] = lags[
                    j2 * block_rows : (j2 + 1) * block_rows, a * LANES : (a + 1) * LANES
                ]
        return carry

    if slots <= 4:
        for s in range(slots):
            one_slot(s, 0)
    else:
        lax.fori_loop(0, slots, one_slot, 0)


def exchange(mine, sizes):
    pairs, sections, subs = sizes
    block = mine.shape[0]
    axes = ("pairs", "section", "sub")
    if (pairs, sections, subs) != (4, 2, 2):
        everything = lax.all_gather(mine, axes, axis=0, tiled=True)
        blocks = []
        for z in range(pairs):
            for s in range(sections):
                for x in range(subs):
                    blocks.append(
                        ((lambda p, q, u, z=z, s=s, x=x: (z, s, x)), ((z * sections + s) * subs + x) * block)
                    )
        return [everything], [blocks]

    def chips(value, *deltas):
        moves = []
        for z in range(pairs):
            for x in range(subs):
                for s in range(sections):
                    dz, dx = deltas[s % len(deltas)]
                    moves.append((((z * sections + s) * subs + x), ((z ^ dz) * sections + s) * subs + (x ^ dx)))
        return lax.ppermute(value, axes, moves)

    def cores(value):
        return lax.ppermute(value, "section", [(0, 1), (1, 0)])

    pieces = [mine]
    plan = [[((lambda p, q, u: (p, q, u)), 0)]]
    other = cores(mine)
    pieces.append(other)
    plan.append([((lambda p, q, u: (p, 1 - q, u)), 0)])
    both = jnp.concatenate([mine, other], axis=0)
    done = {}
    for number in ORDER:
        d0, d1, source = STEPS[number]
        single = source == "own"
        if source == "own":
            carried, f0, f1 = mine, (0, 0), (0, 0)
        elif source == "both":
            carried, f0, f1 = both, (0, 0), (0, 0)
        else:
            carried, f0, f1 = done[source]
            single = carried.shape[0] == block
        arrived = chips(carried, d0, d1)
        d0 = (d0[0] ^ f0[0], d0[1] ^ f0[1])
        d1 = (d1[0] ^ f1[0], d1[1] ^ f1[1])
        done[number] = (arrived, d0, d1)

        def here(p, q, u, d0=d0, d1=d1):
            return (p ^ jnp.where(q == 0, d0[0], d1[0]), q, u ^ jnp.where(q == 0, d0[1], d1[1]))

        def here_flip(p, q, u, here=here):
            z, s, x = here(p, q, u)
            return z, 1 - s, x

        def there(p, q, u, here=here):
            return here(p, 1 - q, u)

        def there_flip(p, q, u, there=there):
            z, s, x = there(p, q, u)
            return z, 1 - s, x

        pieces.append(arrived)
        plan.append([(here, 0)] if single else [(here, 0), (here_flip, block)])
        pieces.append(cores(arrived))
        plan.append([(there, 0)] if single else [(there, 0), (there_flip, block)])
    return pieces, plan


def body(raw_record, fir_taps, channel_ids, offsets, pair_table):
    rows = raw_record.shape[0]
    windows = offsets.shape[0]
    sizes = tuple(lax.axis_size(name) for name in ("pairs", "section", "sub"))
    pairs, sections, subs = sizes
    block_rows = rows * sections
    slots = pair_table.shape[0] // pairs
    a_count = block_rows // (sections * subs)
    vmem = pl.BlockSpec(memory_space=pltpu.VMEM)
    smem = pl.BlockSpec(memory_space=pltpu.SMEM)

    operands = [offsets, fir_taps.reshape(1, TAPS), raw_record]
    operands += [jnp.asarray(c) for c in forward_constants(rows, windows)]
    operands = [pltpu.with_memory_space_constraint(operand, pltpu.HBM) for operand in operands]
    whitened = pl.pallas_call(
        spectra_kernel,
        name="spectra",
        out_shape=pltpu.VMEM((rows * windows * COARSE, LANES), jnp.bfloat16),
        in_specs=[pl.BlockSpec(memory_space=pltpu.HBM)] * len(operands),
        out_specs=vmem,
        scratch_shapes=[pltpu.SMEM(offsets.shape, offsets.dtype)]
        + [pltpu.VMEM(operand.shape, operand.dtype) for operand in operands[1:]]
        + [
            pltpu.VMEM((windows, rows * WINDOW_CHUNKS, LANES), jnp.float32),
            pltpu.VMEM((8, LANES), jnp.float32),
            pltpu.SemaphoreType.DMA((len(operands),)),
        ],
        compiler_params=pltpu.CompilerParams(vmem_limit_bytes=32 * 1024 * 1024),
    )(*operands)

    pieces, plan = exchange(whitened, sizes)

    consts = [jnp.asarray(c) for c in inverse_constants(block_rows)]
    return pl.pallas_call(
        functools.partial(correlate_kernel, plan, sizes),
        name="correlate",
        out_shape=jax.ShapeDtypeStruct((a_count, slots, block_rows, NF), jnp.float32),
        in_specs=[smem, smem] + [vmem] * (3 + len(pieces)),
        out_specs=vmem,
        scratch_shapes=[
            pltpu.VMEM((rows * pairs * sections, windows * subs, COARSE, LANES), jnp.bfloat16),
            pltpu.SMEM((channel_ids.shape[0],), jnp.int32),
        ],
        compiler_params=pltpu.CompilerParams(vmem_limit_bytes=32 * 1024 * 1024),
    )(channel_ids, pair_table, *consts, *pieces)


def solution(mesh):
    return jax.shard_map(
        body,
        mesh=mesh,
        in_specs=(
            P(("groups", "pairs", "section"), "sub"),
            P(),
            P("groups"),
            P(("groups", "sub")),
            P("groups", None),
        ),
        out_specs=P(("section", "sub"), ("groups", "pairs"), None, None),
        check_vma=False,
    )
```

```python
import functools
import math

import jax
import jax.numpy as jnp
import ml_dtypes
import numpy as np
from jax import lax
from jax.experimental import pallas as pl
from jax.experimental.pallas import tpu as pltpu
from jax.sharding import PartitionSpec as P

NF = 2048
TAPS = 64
DEC = 4
BAND = 64
LANES = 128
HALF = LANES // 2
COARSE = NF // LANES

CHUNK_STEP = DEC * LANES // LANES
WINDOW_CHUNKS = CHUNK_STEP * (COARSE - 1) + 6
STEPS = (((1, 0), (1, 0), 'own'), ((2, 0), (2, 1), 'both'), ((3, 0), (3, 1), 'both'), ((0, 1), (1, 1), 'both'))
ORDER = (3, 2, 1, 0)
GRAIN = LANES // DEC


def two_terms(values):
    high = values.astype(ml_dtypes.bfloat16)
    low = (values - high.astype(np.float64)).astype(ml_dtypes.bfloat16)
    return high, low


def forward_constants(rows, windows):
    k1 = np.arange(COARSE)
    fine = np.arange(LANES)
    k2 = np.arange(HALF)
    angle_a = 2 * np.pi * np.outer(k1, np.arange(COARSE)) / COARSE
    count = rows * windows
    blocks = np.zeros((2, rows, windows, COARSE, windows, rows, COARSE))
    for r in range(rows):
        for w in range(windows):
            blocks[0, r, w, :, w, r, :] = np.cos(angle_a)
            blocks[1, r, w, :, w, r, :] = -np.sin(angle_a)
    high, low = two_terms(blocks.reshape(2 * count * COARSE, count * COARSE))
    step_a = np.concatenate([high, low], axis=1)
    angle_t = 2 * np.pi * np.outer(k1, fine) / NF
    twiddle = np.concatenate([np.cos(angle_t), -np.sin(angle_t)], axis=0).astype(np.float32)
    angle_b = 2 * np.pi * np.outer(fine, k2) / LANES
    cos_b, sin_b = np.cos(angle_b), np.sin(angle_b)
    table = np.concatenate(
        [np.concatenate([cos_b, -sin_b], axis=1), np.concatenate([sin_b, cos_b], axis=1)], axis=0
    )
    high, low = two_terms(table)
    step_b = np.concatenate([high, high, low], axis=0)
    band_of = np.tile(k2 * COARSE // BAND, 2)
    same_band = (band_of[:, None] == band_of[None, :]).astype(ml_dtypes.bfloat16)
    return step_a, twiddle, step_b, same_band


def inverse_constants(block_rows):
    k1 = np.arange(COARSE)
    k2 = np.arange(HALF)
    j1 = np.arange(LANES)
    angle_b = 2 * np.pi * np.outer(k2, j1) / LANES
    cos_b, sin_b = np.cos(angle_b), np.sin(angle_b)
    table = np.concatenate(
        [np.concatenate([cos_b, sin_b], axis=1), np.concatenate([-sin_b, cos_b], axis=1)], axis=0
    )
    step_b = np.concatenate(two_terms(table), axis=0)
    sign = np.where(k1 % 2 == 0, 1.0, -1.0)[:, None] / math.sqrt(NF)
    angle_t = 2 * np.pi * np.outer(k1, j1) / NF
    twiddle = np.concatenate([sign * np.cos(angle_t), sign * np.sin(angle_t)], axis=0)
    angle_a = 2 * np.pi * np.outer(np.arange(COARSE), k1) / COARSE
    blocks = np.zeros((COARSE, block_rows, 2, block_rows, COARSE))
    for b in range(block_rows):
        blocks[:, b, 0, b, :] = np.cos(angle_a)
        blocks[:, b, 1, b, :] = -np.sin(angle_a)
    high, low = two_terms(blocks.reshape(COARSE * block_rows, 2 * block_rows * COARSE))
    step_a = np.concatenate([high, high, low], axis=1)
    return step_b, twiddle.astype(np.float32), step_a


def split_terms(values):
    high = values.astype(jnp.bfloat16)
    low = (values - high.astype(jnp.float32)).astype(jnp.bfloat16)
    return high, low


def spectra_kernel(sizes, a_count, *refs):
    half = (len(refs) - 6) // 2
    sources, places = refs[:half], refs[half + 2 : 2 * half + 2]
    out_ref, wanted_ref = refs[half : half + 2]
    chunks, padded, row_of, arrived = refs[2 * half + 2 :]
    raw_ref, offsets_ref, taps_ref, ids_ref, table_ref, step_a_ref, twiddle_ref, step_b_ref, band_ref = places
    copies = [
        pltpu.make_async_copy(source, place, arrived.at[q])
        for q, (source, place) in enumerate(zip(sources, places))
    ]
    for copy in copies:
        copy.start()
    wait_raw, wait_offsets, wait_taps, wait_ids, wait_table, wait_a, wait_t, wait_b, wait_band = [
        copy.wait for copy in copies
    ]
    rows = raw_ref.shape[0]
    windows = offsets_ref.shape[0]
    count = rows * windows
    chunk_total = raw_ref.shape[1] // LANES
    padded[...] = jnp.zeros_like(padded)
    wait_taps()
    padded[0:1, 0:TAPS] = taps_ref[...]
    plain = jnp.broadcast_to(padded[0:1, :], padded.shape)
    sublane = lax.broadcasted_iota(jnp.int32, padded.shape, 0)
    stair = plain
    for i in range(1, 8):
        stair = jnp.where(sublane == i, pltpu.roll(plain, DEC * i, 1), stair)
    stair = jnp.concatenate([stair, jnp.zeros((8, 2 * LANES), jnp.float32)], axis=1)
    empty = jnp.zeros((GRAIN, LANES), jnp.float32)
    wait_offsets()
    starts, filters = [], []
    for w in range(windows):
        start = offsets_ref[w]
        first = jnp.minimum(start // LANES, chunk_total - WINDOW_CHUNKS)
        shift = start - first * LANES
        starts.append(pl.multiple_of(first * LANES, LANES))
        band = jnp.concatenate(
            [pltpu.roll(stair, shift + 8 * DEC * g, 1) for g in range(GRAIN // 8)], axis=0
        )
        columns = []
        for m in range(6):
            column = [
                band[:, (m - g) * LANES : (m - g + 1) * LANES] if 0 <= m - g < 3 else empty
                for g in range(DEC)
            ]
            columns.append(jnp.concatenate(column, axis=0))
        filters.append(jnp.concatenate(split_terms(jnp.concatenate(columns, axis=1)), axis=0))
    for wait in (wait_raw, wait_ids, wait_table, wait_a, wait_t, wait_b, wait_band):
        wait()
    parts = []
    for w in range(windows):
        slab = raw_ref[:, pl.ds(starts[w], WINDOW_CHUNKS * LANES)].astype(jnp.float32)
        for c in range(WINDOW_CHUNKS):
            chunks[w, rows * c : rows * (c + 1), :] = slab[:, c * LANES : (c + 1) * LANES]
        left = []
        for m in range(6):
            pieces = [
                chunks[w, pl.ds(rows * m + r, COARSE, stride=rows * CHUNK_STEP), :] for r in range(rows)
            ]
            left.append(jnp.concatenate(pieces, axis=0).astype(jnp.bfloat16))
        both = lax.dot_general(
            jnp.concatenate(left, axis=1),
            filters[w],
            (((1,), (1,)), ((), ())),
            preferred_element_type=jnp.float32,
        )
        parts.append((both[:, :LANES] + both[:, LANES:]).astype(jnp.bfloat16))
    decimated = jnp.concatenate(parts, axis=0)
    pairs, _, subs = sizes
    channels = ids_ref.shape[0]
    slots = table_ref.shape[1] // pairs
    block_rows = a_count * sizes[1] * subs
    my_pair = lax.axis_index("pairs")
    first_a = (lax.axis_index("section") * subs + lax.axis_index("sub")) * a_count
    for c in range(channels):
        row_of[ids_ref[c]] = c
    width = 1 + a_count + block_rows
    for s in range(slots):
        first_block = table_ref[0, my_pair * slots + s]
        second_block = table_ref[1, my_pair * slots + s]
        wanted_ref[s * width] = first_block
        first_block = jnp.maximum(first_block, 0) * block_rows + first_a
        second_block = jnp.maximum(second_block, 0) * block_rows
        for a in range(a_count):
            wanted_ref[s * width + 1 + a] = row_of[first_block + a]
        for b in range(block_rows):
            wanted_ref[s * width + 1 + a_count + b] = row_of[second_block + b]
    coarse = jnp.dot(
        step_a_ref[...], jnp.concatenate([decimated, decimated], axis=0), preferred_element_type=jnp.float32
    )
    size = count * COARSE
    real = coarse[:size].reshape(count, COARSE, LANES)
    imag = coarse[size:].reshape(count, COARSE, LANES)
    cos_t = twiddle_ref[:COARSE][None]
    sin_t = twiddle_ref[COARSE:][None]
    turned = jnp.concatenate(
        [
            (real * cos_t - imag * sin_t).reshape(size, LANES),
            (real * sin_t + imag * cos_t).reshape(size, LANES),
        ],
        axis=1,
    )
    high, low = split_terms(turned)
    spectrum = jnp.dot(
        jnp.concatenate([high, low, high], axis=1), step_b_ref[...], preferred_element_type=jnp.float32
    ).reshape(count, COARSE, LANES)
    power = jnp.sum(spectrum * spectrum, axis=1)
    high, low = split_terms(power)
    banded = jnp.dot(high, band_ref[...], preferred_element_type=jnp.float32) + jnp.dot(
        low, band_ref[...], preferred_element_type=jnp.float32
    )
    inverse_rms = lax.rsqrt(banded * (1.0 / BAND) + 1e-06)
    out_ref[...] = (spectrum * inverse_rms[:, None, :]).reshape(size, LANES).astype(jnp.bfloat16)


def correlate_kernel(
    plan, groups_of, wanted_ref, step_b_ref, twiddle_ref, step_a_ref, *refs
):
    piece_refs = refs[: len(plan)]
    out_ref, gathered, staged, sent = refs[len(plan) :]
    pairs, sections, subs = groups_of
    a_count, slots, block_rows = staged.shape[:3]
    rows_total, windows_total = gathered.shape[:2]
    rows = rows_total // (pairs * sections)
    windows = windows_total // subs
    tile = rows * windows * COARSE
    my_pair = lax.axis_index("pairs")
    my_section = lax.axis_index("section")
    my_sub = lax.axis_index("sub")

    for ref, blocks in zip(piece_refs, plan):
        for q, (locate, offset) in enumerate(blocks):
            pair, section, sub = locate(my_pair, my_section, my_sub)
            base_row = (pair * sections + section) * rows
            base_window = sub * windows
            for r in range(rows):
                for w in range(windows):
                    at = offset + (r * windows + w) * COARSE
                    gathered[base_row + r, base_window + w] = ref[at : at + COARSE, :]

    lane = lax.broadcasted_iota(jnp.int32, (COARSE, LANES), 1)
    coarse_bin = lax.broadcasted_iota(jnp.int32, (COARSE, LANES), 0)
    in_left = lane < HALF
    is_zero_bin = (coarse_bin == 0) & (lane % HALF == 0)
    weight = jnp.where(is_zero_bin, 1.0, 2.0) * (1.0 / windows_total)
    cos_t = twiddle_ref[:COARSE][None]
    sin_t = twiddle_ref[COARSE:][None]
    size = block_rows * COARSE
    width = 1 + a_count + block_rows

    def write_out(s):
        return pltpu.make_async_copy(staged.at[:, s], out_ref.at[:, s], sent.at[s])

    def one_slot(s, carry):
        live = jnp.where(wanted_ref[s * width] >= 0, 1.0, 0.0)
        scale = weight * live
        ones, turns = [], []
        for a in range(a_count):
            row = wanted_ref[s * width + 1 + a]
            one = [gathered[row, w].astype(jnp.float32) for w in range(windows_total)]
            ones.append(one)
            turns.append([jnp.where(in_left, 1.0, -1.0) * pltpu.roll(v, HALF, 1) for v in one])
        crosses = [[] for _ in range(a_count)]
        for b in range(block_rows):
            row = wanted_ref[s * width + 1 + a_count + b]
            other = [gathered[row, w].astype(jnp.float32) for w in range(windows_total)]
            for a in range(a_count):
                even = ones[a][0] * other[0]
                odd = turns[a][0] * other[0]
                for w in range(1, windows_total):
                    even = even + ones[a][w] * other[w]
                    odd = odd + turns[a][w] * other[w]
                cross = jnp.where(in_left, even, odd) + pltpu.roll(jnp.where(in_left, odd, even), HALF, 1)
                crosses[a].append((cross * scale).astype(jnp.bfloat16))
        cross = jnp.concatenate([c for per_a in crosses for c in per_a], axis=0)
        fine = jnp.dot(
            jnp.concatenate([cross, cross], axis=1), step_b_ref[...], preferred_element_type=jnp.float32
        ).reshape(a_count * block_rows, COARSE, 2 * LANES)
        real, imag = fine[:, :, :LANES], fine[:, :, LANES:]
        turned_real = (real * cos_t - imag * sin_t).reshape(a_count, size, LANES)
        turned_imag = (real * sin_t + imag * cos_t).reshape(a_count, size, LANES)
        turned = jnp.concatenate(
            [
                jnp.concatenate([turned_real[a] for a in range(a_count)], axis=1),
                jnp.concatenate([turned_imag[a] for a in range(a_count)], axis=1),
            ],
            axis=0,
        )
        return split_terms(turned)

    def finish(s, turned):
        high, low = turned
        lags = jnp.dot(
            step_a_ref[...], jnp.concatenate([high, low, high], axis=0), preferred_element_type=jnp.float32
        )
        for a in range(a_count):
            for j2 in range(COARSE):
                staged[a, s, :, j2 * LANES : (j2 + 1) * LANES] = lags[
                    j2 * block_rows : (j2 + 1) * block_rows, a * LANES : (a + 1) * LANES
                ]
        write_out(s).start()

    def whole_slot(s, carry):
        finish(s, one_slot(s, 0))
        return carry

    if slots <= 4:
        kept = [one_slot(s, 0) for s in range(slots)]
        for s in range(slots):
            finish(s, kept[s])
    else:
        lax.fori_loop(0, slots, whole_slot, 0)
    for s in range(slots):
        write_out(s).wait()


def exchange(mine, sizes):
    pairs, sections, subs = sizes
    block = mine.shape[0]
    axes = ("pairs", "section", "sub")
    if (pairs, sections, subs) != (4, 2, 2):
        everything = lax.all_gather(mine, axes, axis=0, tiled=True)
        blocks = []
        for z in range(pairs):
            for s in range(sections):
                for x in range(subs):
                    blocks.append(
                        ((lambda p, q, u, z=z, s=s, x=x: (z, s, x)), ((z * sections + s) * subs + x) * block)
                    )
        return [everything], [blocks]

    def chips(value, *deltas):
        moves = []
        for z in range(pairs):
            for x in range(subs):
                for s in range(sections):
                    dz, dx = deltas[s % len(deltas)]
                    moves.append((((z * sections + s) * subs + x), ((z ^ dz) * sections + s) * subs + (x ^ dx)))
        return lax.ppermute(value, axes, moves)

    def cores(value):
        return lax.ppermute(value, "section", [(0, 1), (1, 0)])

    pieces = [mine]
    plan = [[((lambda p, q, u: (p, q, u)), 0)]]
    other = cores(mine)
    pieces.append(other)
    plan.append([((lambda p, q, u: (p, 1 - q, u)), 0)])
    both = jnp.concatenate([mine, other], axis=0)
    done = {}
    for number in ORDER:
        d0, d1, source = STEPS[number]
        single = source == "own"
        if source == "own":
            carried, f0, f1 = mine, (0, 0), (0, 0)
        elif source == "both":
            carried, f0, f1 = both, (0, 0), (0, 0)
        else:
            carried, f0, f1 = done[source]
            single = carried.shape[0] == block
        arrived = chips(carried, d0, d1)
        d0 = (d0[0] ^ f0[0], d0[1] ^ f0[1])
        d1 = (d1[0] ^ f1[0], d1[1] ^ f1[1])
        done[number] = (arrived, d0, d1)

        def here(p, q, u, d0=d0, d1=d1):
            return (p ^ jnp.where(q == 0, d0[0], d1[0]), q, u ^ jnp.where(q == 0, d0[1], d1[1]))

        def here_flip(p, q, u, here=here):
            z, s, x = here(p, q, u)
            return z, 1 - s, x

        def there(p, q, u, here=here):
            return here(p, 1 - q, u)

        def there_flip(p, q, u, there=there):
            z, s, x = there(p, q, u)
            return z, 1 - s, x

        pieces.append(arrived)
        plan.append([(here, 0)] if single else [(here, 0), (here_flip, block)])
        pieces.append(cores(arrived))
        plan.append([(there, 0)] if single else [(there, 0), (there_flip, block)])
    return pieces, plan


def body(raw_record, fir_taps, channel_ids, offsets, pair_table):
    rows = raw_record.shape[0]
    windows = offsets.shape[0]
    sizes = tuple(lax.axis_size(name) for name in ("pairs", "section", "sub"))
    pairs, sections, subs = sizes
    block_rows = rows * sections
    slots = pair_table.shape[0] // pairs
    a_count = block_rows // (sections * subs)
    vmem = pl.BlockSpec(memory_space=pltpu.VMEM)
    smem = pl.BlockSpec(memory_space=pltpu.SMEM)

    operands = [raw_record, offsets, fir_taps.reshape(1, TAPS), channel_ids, pair_table.T]
    operands += [jnp.asarray(c) for c in forward_constants(rows, windows)]
    operands = [pltpu.with_memory_space_constraint(operand, pltpu.HBM) for operand in operands]
    in_scalar = (1, 3, 4)
    wanted_count = slots * (1 + a_count + block_rows)
    whitened, wanted = pl.pallas_call(
        functools.partial(spectra_kernel, sizes, a_count),
        name="spectra",
        out_shape=(
            pltpu.VMEM((rows * windows * COARSE, LANES), jnp.bfloat16),
            pltpu.SMEM((wanted_count,), jnp.int32),
        ),
        in_specs=[pl.BlockSpec(memory_space=pltpu.HBM)] * len(operands),
        out_specs=(vmem, smem),
        scratch_shapes=[
            (pltpu.SMEM if q in in_scalar else pltpu.VMEM)(operand.shape, operand.dtype)
            for q, operand in enumerate(operands)
        ]
        + [
            pltpu.VMEM((windows, rows * WINDOW_CHUNKS, LANES), jnp.float32),
            pltpu.VMEM((8, LANES), jnp.float32),
            pltpu.SMEM(channel_ids.shape, jnp.int32),
            pltpu.SemaphoreType.DMA((len(operands),)),
        ],
        compiler_params=pltpu.CompilerParams(vmem_limit_bytes=32 * 1024 * 1024),
    )(*operands)

    pieces, plan = exchange(whitened, sizes)

    wanted = pltpu.with_memory_space_constraint(wanted, pltpu.SMEM)
    consts = [jnp.asarray(c) for c in inverse_constants(block_rows)]
    result = (a_count, slots, block_rows, NF)
    return pl.pallas_call(
        functools.partial(correlate_kernel, plan, sizes),
        name="correlate",
        out_shape=jax.ShapeDtypeStruct(result, jnp.float32),
        in_specs=[smem] + [vmem] * (3 + len(pieces)),
        out_specs=pl.BlockSpec(memory_space=pltpu.HBM),
        scratch_shapes=[
            pltpu.VMEM((rows * pairs * sections, windows * subs, COARSE, LANES), jnp.bfloat16),
            pltpu.VMEM(result, jnp.float32),
            pltpu.SemaphoreType.DMA((slots,)),
        ],
        compiler_params=pltpu.CompilerParams(vmem_limit_bytes=32 * 1024 * 1024),
    )(wanted, *consts, *pieces)


def solution(mesh):
    return jax.shard_map(
        body,
        mesh=mesh,
        in_specs=(
            P(("groups", "pairs", "section"), "sub"),
            P(),
            P("groups"),
            P(("groups", "sub")),
            P("groups", None),
        ),
        out_specs=P(("section", "sub"), ("groups", "pairs"), None, None),
        check_vma=False,
    )
```

```python
import functools
import math

import jax
import jax.numpy as jnp
import ml_dtypes
import numpy as np
from jax import lax
from jax.experimental import pallas as pl
from jax.experimental.pallas import tpu as pltpu
from jax.sharding import PartitionSpec as P

NF = 2048
TAPS = 64
DEC = 4
BAND = 64
LANES = 128
HALF = LANES // 2
COARSE = NF // LANES

CHUNK_STEP = DEC * LANES // LANES
WINDOW_CHUNKS = CHUNK_STEP * (COARSE - 1) + 6
ROUNDS = (
    ((0, 1), (1, 1), "both"),
    ((1, 0), (1, 0), "own"),
    ((3, 0), (3, 1), "both"),
    ((2, 0), (2, 1), "both"),
)
GRAIN = LANES // DEC


def two_terms(values):
    high = values.astype(ml_dtypes.bfloat16)
    low = (values - high.astype(np.float64)).astype(ml_dtypes.bfloat16)
    return high, low


def forward_constants(rows, windows):
    k1 = np.arange(COARSE)
    fine = np.arange(LANES)
    k2 = np.arange(HALF)
    angle_a = 2 * np.pi * np.outer(k1, np.arange(COARSE)) / COARSE
    count = rows * windows
    blocks = np.zeros((2, rows, windows, COARSE, windows, rows, COARSE))
    for r in range(rows):
        for w in range(windows):
            blocks[0, r, w, :, w, r, :] = np.cos(angle_a)
            blocks[1, r, w, :, w, r, :] = -np.sin(angle_a)
    high, low = two_terms(blocks.reshape(2 * count * COARSE, count * COARSE))
    step_a = np.concatenate([high, low], axis=1)
    angle_t = 2 * np.pi * np.outer(k1, fine) / NF
    twiddle = np.concatenate([np.cos(angle_t), -np.sin(angle_t)], axis=0).astype(np.float32)
    angle_b = 2 * np.pi * np.outer(fine, k2) / LANES
    cos_b, sin_b = np.cos(angle_b), np.sin(angle_b)
    table = np.concatenate(
        [np.concatenate([cos_b, -sin_b], axis=1), np.concatenate([sin_b, cos_b], axis=1)], axis=0
    )
    high, low = two_terms(table)
    step_b = np.concatenate([high, high, low], axis=0)
    band_of = np.tile(k2 * COARSE // BAND, 2)
    same_band = (band_of[:, None] == band_of[None, :]).astype(ml_dtypes.bfloat16)
    return step_a, twiddle, step_b, same_band


def inverse_constants(block_rows):
    k1 = np.arange(COARSE)
    k2 = np.arange(HALF)
    j1 = np.arange(LANES)
    angle_b = 2 * np.pi * np.outer(k2, j1) / LANES
    cos_b, sin_b = np.cos(angle_b), np.sin(angle_b)
    table = np.concatenate(
        [np.concatenate([cos_b, sin_b], axis=1), np.concatenate([-sin_b, cos_b], axis=1)], axis=0
    )
    step_b = np.concatenate(two_terms(table), axis=0)
    sign = np.where(k1 % 2 == 0, 1.0, -1.0)[:, None] / math.sqrt(NF)
    angle_t = 2 * np.pi * np.outer(k1, j1) / NF
    twiddle = np.concatenate([sign * np.cos(angle_t), sign * np.sin(angle_t)], axis=0)
    angle_a = 2 * np.pi * np.outer(np.arange(COARSE), k1) / COARSE
    blocks = np.zeros((COARSE, block_rows, 2, block_rows, COARSE))
    for b in range(block_rows):
        blocks[:, b, 0, b, :] = np.cos(angle_a)
        blocks[:, b, 1, b, :] = -np.sin(angle_a)
    high, low = two_terms(blocks.reshape(COARSE * block_rows, 2 * block_rows * COARSE))
    step_a = np.concatenate([high, high, low], axis=1)
    return step_b, twiddle.astype(np.float32), step_a


def split_terms(values):
    high = values.astype(jnp.bfloat16)
    low = (values - high.astype(jnp.float32)).astype(jnp.bfloat16)
    return high, low


def spectra_kernel(sizes, a_count, *refs):
    half = (len(refs) - 6) // 2
    sources, places = refs[:half], refs[half + 2 : 2 * half + 2]
    out_ref, wanted_ref = refs[half : half + 2]
    chunks, padded, row_of, arrived = refs[2 * half + 2 :]
    raw_ref, offsets_ref, taps_ref, ids_ref, table_ref, step_a_ref, twiddle_ref, step_b_ref, band_ref = places
    copies = [
        pltpu.make_async_copy(source, place, arrived.at[q])
        for q, (source, place) in enumerate(zip(sources, places))
    ]
    for copy in copies:
        copy.start()
    wait_raw, wait_offsets, wait_taps, wait_ids, wait_table, wait_a, wait_t, wait_b, wait_band = [
        copy.wait for copy in copies
    ]
    rows = raw_ref.shape[0]
    windows = offsets_ref.shape[0]
    count = rows * windows
    chunk_total = raw_ref.shape[1] // LANES
    padded[...] = jnp.zeros_like(padded)
    wait_taps()
    padded[0:1, 0:TAPS] = taps_ref[...]
    plain = jnp.broadcast_to(padded[0:1, :], padded.shape)
    sublane = lax.broadcasted_iota(jnp.int32, padded.shape, 0)
    stair = plain
    for i in range(1, 8):
        stair = jnp.where(sublane == i, pltpu.roll(plain, DEC * i, 1), stair)
    stair = jnp.concatenate([stair, jnp.zeros((8, 2 * LANES), jnp.float32)], axis=1)
    empty = jnp.zeros((GRAIN, LANES), jnp.float32)
    wait_offsets()
    starts, filters = [], []
    for w in range(windows):
        start = offsets_ref[w]
        first = jnp.minimum(start // LANES, chunk_total - WINDOW_CHUNKS)
        shift = start - first * LANES
        starts.append(pl.multiple_of(first * LANES, LANES))
        band = jnp.concatenate(
            [pltpu.roll(stair, shift + 8 * DEC * g, 1) for g in range(GRAIN // 8)], axis=0
        )
        columns = []
        for m in range(6):
            column = [
                band[:, (m - g) * LANES : (m - g + 1) * LANES] if 0 <= m - g < 3 else empty
                for g in range(DEC)
            ]
            columns.append(jnp.concatenate(column, axis=0))
        filters.append(jnp.concatenate(split_terms(jnp.concatenate(columns, axis=1)), axis=0))
    for wait in (wait_raw, wait_ids, wait_table, wait_a, wait_t, wait_b, wait_band):
        wait()
    parts = []
    for w in range(windows):
        slab = raw_ref[:, pl.ds(starts[w], WINDOW_CHUNKS * LANES)].astype(jnp.float32)
        for c in range(WINDOW_CHUNKS):
            chunks[w, rows * c : rows * (c + 1), :] = slab[:, c * LANES : (c + 1) * LANES]
        left = []
        for m in range(6):
            pieces = [
                chunks[w, pl.ds(rows * m + r, COARSE, stride=rows * CHUNK_STEP), :] for r in range(rows)
            ]
            left.append(jnp.concatenate(pieces, axis=0).astype(jnp.bfloat16))
        both = lax.dot_general(
            jnp.concatenate(left, axis=1),
            filters[w],
            (((1,), (1,)), ((), ())),
            preferred_element_type=jnp.float32,
        )
        parts.append((both[:, :LANES] + both[:, LANES:]).astype(jnp.bfloat16))
    decimated = jnp.concatenate(parts, axis=0)
    pairs, _, subs = sizes
    channels = ids_ref.shape[0]
    slots = table_ref.shape[1] // pairs
    block_rows = a_count * sizes[1] * subs
    my_pair = lax.axis_index("pairs")
    first_a = (lax.axis_index("section") * subs + lax.axis_index("sub")) * a_count
    for c in range(channels):
        row_of[ids_ref[c]] = c
    width = 1 + a_count + block_rows
    for s in range(slots):
        first_block = table_ref[0, my_pair * slots + s]
        second_block = table_ref[1, my_pair * slots + s]
        wanted_ref[s * width] = first_block
        first_block = jnp.maximum(first_block, 0) * block_rows + first_a
        second_block = jnp.maximum(second_block, 0) * block_rows
        for a in range(a_count):
            wanted_ref[s * width + 1 + a] = row_of[first_block + a]
        for b in range(block_rows):
            wanted_ref[s * width + 1 + a_count + b] = row_of[second_block + b]
    coarse = jnp.dot(
        step_a_ref[...], jnp.concatenate([decimated, decimated], axis=0), preferred_element_type=jnp.float32
    )
    size = count * COARSE
    real = coarse[:size].reshape(count, COARSE, LANES)
    imag = coarse[size:].reshape(count, COARSE, LANES)
    cos_t = twiddle_ref[:COARSE][None]
    sin_t = twiddle_ref[COARSE:][None]
    turned = jnp.concatenate(
        [
            (real * cos_t - imag * sin_t).reshape(size, LANES),
            (real * sin_t + imag * cos_t).reshape(size, LANES),
        ],
        axis=1,
    )
    high, low = split_terms(turned)
    spectrum = jnp.dot(
        jnp.concatenate([high, low, high], axis=1), step_b_ref[...], preferred_element_type=jnp.float32
    ).reshape(count, COARSE, LANES)
    power = jnp.sum(spectrum * spectrum, axis=1)
    high, low = split_terms(power)
    banded = jnp.dot(high, band_ref[...], preferred_element_type=jnp.float32) + jnp.dot(
        low, band_ref[...], preferred_element_type=jnp.float32
    )
    inverse_rms = lax.rsqrt(banded * (1.0 / BAND) + 1e-06)
    out_ref[...] = (spectrum * inverse_rms[:, None, :]).reshape(size, LANES).astype(jnp.bfloat16)


def correlate_kernel(
    plan, groups_of, wanted_ref, step_b_ref, twiddle_ref, step_a_ref, *refs
):
    piece_refs = refs[: len(plan)]
    out_ref, gathered, staged, sent = refs[len(plan) :]
    pairs, sections, subs = groups_of
    a_count, slots, block_rows = staged.shape[:3]
    rows_total, windows_total = gathered.shape[:2]
    rows = rows_total // (pairs * sections)
    windows = windows_total // subs
    tile = rows * windows * COARSE
    my_pair = lax.axis_index("pairs")
    my_section = lax.axis_index("section")
    my_sub = lax.axis_index("sub")

    for ref, blocks in zip(piece_refs, plan):
        for q, (locate, offset) in enumerate(blocks):
            pair, section, sub = locate(my_pair, my_section, my_sub)
            base_row = (pair * sections + section) * rows
            base_window = sub * windows
            for r in range(rows):
                for w in range(windows):
                    at = offset + (r * windows + w) * COARSE
                    gathered[base_row + r, base_window + w] = ref[at : at + COARSE, :]

    lane = lax.broadcasted_iota(jnp.int32, (COARSE, LANES), 1)
    coarse_bin = lax.broadcasted_iota(jnp.int32, (COARSE, LANES), 0)
    in_left = lane < HALF
    is_zero_bin = (coarse_bin == 0) & (lane % HALF == 0)
    weight = jnp.where(is_zero_bin, 1.0, 2.0) * (1.0 / windows_total)
    cos_t = twiddle_ref[:COARSE][None]
    sin_t = twiddle_ref[COARSE:][None]
    size = block_rows * COARSE
    width = 1 + a_count + block_rows

    def write_out(s):
        return pltpu.make_async_copy(staged.at[:, s], out_ref.at[:, s], sent.at[s])

    def one_slot(s, carry):
        live = jnp.where(wanted_ref[s * width] >= 0, 1.0, 0.0)
        scale = weight * live
        ones, turns = [], []
        for a in range(a_count):
            row = wanted_ref[s * width + 1 + a]
            one = [gathered[row, w].astype(jnp.float32) for w in range(windows_total)]
            ones.append(one)
            turns.append([jnp.where(in_left, 1.0, -1.0) * pltpu.roll(v, HALF, 1) for v in one])
        crosses = [[] for _ in range(a_count)]
        for b in range(block_rows):
            row = wanted_ref[s * width + 1 + a_count + b]
            other = [gathered[row, w].astype(jnp.float32) for w in range(windows_total)]
            for a in range(a_count):
                even = ones[a][0] * other[0]
                odd = turns[a][0] * other[0]
                for w in range(1, windows_total):
                    even = even + ones[a][w] * other[w]
                    odd = odd + turns[a][w] * other[w]
                cross = jnp.where(in_left, even, odd) + pltpu.roll(jnp.where(in_left, odd, even), HALF, 1)
                crosses[a].append((cross * scale).astype(jnp.bfloat16))
        cross = jnp.concatenate([c for per_a in crosses for c in per_a], axis=0)
        fine = jnp.dot(
            jnp.concatenate([cross, cross], axis=1), step_b_ref[...], preferred_element_type=jnp.float32
        ).reshape(a_count * block_rows, COARSE, 2 * LANES)
        real, imag = fine[:, :, :LANES], fine[:, :, LANES:]
        turned_real = (real * cos_t - imag * sin_t).reshape(a_count, size, LANES)
        turned_imag = (real * sin_t + imag * cos_t).reshape(a_count, size, LANES)
        turned = jnp.concatenate(
            [
                jnp.concatenate([turned_real[a] for a in range(a_count)], axis=1),
                jnp.concatenate([turned_imag[a] for a in range(a_count)], axis=1),
            ],
            axis=0,
        )
        return turned.astype(jnp.bfloat16), None

    def finish(s, turned):
        high, low = turned
        lags = jnp.dot(
            step_a_ref[:, : 2 * size], high, preferred_element_type=jnp.float32
        )
        for a in range(a_count):
            for j2 in range(COARSE):
                staged[a, s, :, j2 * LANES : (j2 + 1) * LANES] = lags[
                    j2 * block_rows : (j2 + 1) * block_rows, a * LANES : (a + 1) * LANES
                ]
        write_out(s).start()

    def whole_slot(s, carry):
        finish(s, one_slot(s, 0))
        return carry

    if slots <= 4:
        kept = [one_slot(s, 0) for s in range(slots)]
        for s in range(slots):
            finish(s, kept[s])
    else:
        lax.fori_loop(0, slots, whole_slot, 0)
    for s in range(slots):
        write_out(s).wait()


def exchange(mine, sizes):
    pairs, sections, subs = sizes
    block = mine.shape[0]
    axes = ("pairs", "section", "sub")
    if (pairs, sections, subs) != (4, 2, 2):
        everything = lax.all_gather(mine, axes, axis=0, tiled=True)
        blocks = []
        for z in range(pairs):
            for s in range(sections):
                for x in range(subs):
                    blocks.append(
                        ((lambda p, q, u, z=z, s=s, x=x: (z, s, x)), ((z * sections + s) * subs + x) * block)
                    )
        return [everything], [blocks]

    def chips(value, *deltas):
        moves = []
        for z in range(pairs):
            for x in range(subs):
                for s in range(sections):
                    dz, dx = deltas[s % len(deltas)]
                    moves.append((((z * sections + s) * subs + x), ((z ^ dz) * sections + s) * subs + (x ^ dx)))
        return lax.ppermute(value, axes, moves)

    def cores(value):
        return lax.ppermute(value, "section", [(0, 1), (1, 0)])

    pieces = [mine]
    plan = [[((lambda p, q, u: (p, q, u)), 0)]]
    other = cores(mine)
    pieces.append(other)
    plan.append([((lambda p, q, u: (p, 1 - q, u)), 0)])
    both = jnp.concatenate([mine, other], axis=0)
    for d0, d1, source in ROUNDS:
        single = source == "own"
        arrived = chips(mine if single else both, d0, d1)

        def here(p, q, u, d0=d0, d1=d1):
            return (p ^ jnp.where(q == 0, d0[0], d1[0]), q, u ^ jnp.where(q == 0, d0[1], d1[1]))

        def here_flip(p, q, u, here=here):
            z, s, x = here(p, q, u)
            return z, 1 - s, x

        def there(p, q, u, here=here):
            return here(p, 1 - q, u)

        def there_flip(p, q, u, there=there):
            z, s, x = there(p, q, u)
            return z, 1 - s, x

        pieces.append(arrived)
        plan.append([(here, 0)] if single else [(here, 0), (here_flip, block)])
        pieces.append(cores(arrived))
        plan.append([(there, 0)] if single else [(there, 0), (there_flip, block)])
    return pieces, plan


def body(raw_record, fir_taps, channel_ids, offsets, pair_table):
    rows = raw_record.shape[0]
    windows = offsets.shape[0]
    sizes = tuple(lax.axis_size(name) for name in ("pairs", "section", "sub"))
    pairs, sections, subs = sizes
    block_rows = rows * sections
    slots = pair_table.shape[0] // pairs
    a_count = block_rows // (sections * subs)
    vmem = pl.BlockSpec(memory_space=pltpu.VMEM)
    smem = pl.BlockSpec(memory_space=pltpu.SMEM)

    operands = [raw_record, offsets, fir_taps.reshape(1, TAPS), channel_ids, pair_table.T]
    operands += [jnp.asarray(c) for c in forward_constants(rows, windows)]
    operands = [pltpu.with_memory_space_constraint(operand, pltpu.HBM) for operand in operands]
    in_scalar = (1, 3, 4)
    wanted_count = slots * (1 + a_count + block_rows)
    whitened, wanted = pl.pallas_call(
        functools.partial(spectra_kernel, sizes, a_count),
        name="spectra",
        out_shape=(
            pltpu.VMEM((rows * windows * COARSE, LANES), jnp.bfloat16),
            pltpu.SMEM((wanted_count,), jnp.int32),
        ),
        in_specs=[pl.BlockSpec(memory_space=pltpu.HBM)] * len(operands),
        out_specs=(vmem, smem),
        scratch_shapes=[
            (pltpu.SMEM if q in in_scalar else pltpu.VMEM)(operand.shape, operand.dtype)
            for q, operand in enumerate(operands)
        ]
        + [
            pltpu.VMEM((windows, rows * WINDOW_CHUNKS, LANES), jnp.float32),
            pltpu.VMEM((8, LANES), jnp.float32),
            pltpu.SMEM(channel_ids.shape, jnp.int32),
            pltpu.SemaphoreType.DMA((len(operands),)),
        ],
        compiler_params=pltpu.CompilerParams(vmem_limit_bytes=32 * 1024 * 1024),
    )(*operands)

    pieces, plan = exchange(whitened, sizes)

    wanted = pltpu.with_memory_space_constraint(wanted, pltpu.SMEM)
    consts = [jnp.asarray(c) for c in inverse_constants(block_rows)]
    result = (a_count, slots, block_rows, NF)
    return pl.pallas_call(
        functools.partial(correlate_kernel, plan, sizes),
        name="correlate",
        out_shape=jax.ShapeDtypeStruct(result, jnp.float32),
        in_specs=[smem] + [vmem] * (3 + len(pieces)),
        out_specs=pl.BlockSpec(memory_space=pltpu.HBM),
        scratch_shapes=[
            pltpu.VMEM((rows * pairs * sections, windows * subs, COARSE, LANES), jnp.bfloat16),
            pltpu.VMEM(result, jnp.float32),
            pltpu.SemaphoreType.DMA((slots,)),
        ],
        compiler_params=pltpu.CompilerParams(vmem_limit_bytes=32 * 1024 * 1024),
    )(wanted, *consts, *pieces)


def solution(mesh):
    return jax.shard_map(
        body,
        mesh=mesh,
        in_specs=(
            P(("groups", "pairs", "section"), "sub"),
            P(),
            P("groups"),
            P(("groups", "sub")),
            P("groups", None),
        ),
        out_specs=P(("section", "sub"), ("groups", "pairs"), None, None),
        check_vma=False,
    )
```

```python
import functools
import math

import jax
import jax.numpy as jnp
import ml_dtypes
import numpy as np
from jax import lax
from jax.experimental import pallas as pl
from jax.experimental.pallas import tpu as pltpu
from jax.sharding import PartitionSpec as P

NF = 2048
TAPS = 64
DEC = 4
BAND = 64
LANES = 128
HALF = LANES // 2
COARSE = NF // LANES

CHUNK_STEP = DEC * LANES // LANES
WINDOW_CHUNKS = CHUNK_STEP * (COARSE - 1) + 6
ROUNDS = (
    ((0, 1), (1, 1)),
    ((1, 0), (1, 0)),
    ((3, 0), (3, 1)),
    ((2, 0), (2, 1)),
)
GRAIN = LANES // DEC


def two_terms(values):
    high = values.astype(ml_dtypes.bfloat16)
    low = (values - high.astype(np.float64)).astype(ml_dtypes.bfloat16)
    return high, low


def forward_constants(rows, windows):
    k1 = np.arange(COARSE)
    fine = np.arange(LANES)
    k2 = np.arange(HALF)
    angle_a = 2 * np.pi * np.outer(k1, np.arange(COARSE)) / COARSE
    count = rows * windows
    blocks = np.zeros((2, rows, windows, COARSE, windows, rows, COARSE))
    for r in range(rows):
        for w in range(windows):
            blocks[0, r, w, :, w, r, :] = np.cos(angle_a)
            blocks[1, r, w, :, w, r, :] = -np.sin(angle_a)
    high, low = two_terms(blocks.reshape(2 * count * COARSE, count * COARSE))
    step_a = np.concatenate([high, low], axis=1)
    angle_t = 2 * np.pi * np.outer(k1, fine) / NF
    twiddle = np.concatenate([np.cos(angle_t), -np.sin(angle_t)], axis=0).astype(np.float32)
    angle_b = 2 * np.pi * np.outer(fine, k2) / LANES
    cos_b, sin_b = np.cos(angle_b), np.sin(angle_b)
    table = np.concatenate(
        [np.concatenate([cos_b, -sin_b], axis=1), np.concatenate([sin_b, cos_b], axis=1)], axis=0
    )
    high, low = two_terms(table)
    step_b = np.concatenate([high, high, low], axis=0)
    band_of = np.tile(k2 * COARSE // BAND, 2)
    same_band = (band_of[:, None] == band_of[None, :]).astype(ml_dtypes.bfloat16)
    return step_a, twiddle, step_b, same_band


def inverse_constants(block_rows):
    k1 = np.arange(COARSE)
    k2 = np.arange(HALF)
    j1 = np.arange(LANES)
    angle_b = 2 * np.pi * np.outer(k2, j1) / LANES
    cos_b, sin_b = np.cos(angle_b), np.sin(angle_b)
    table = np.concatenate(
        [np.concatenate([cos_b, sin_b], axis=1), np.concatenate([-sin_b, cos_b], axis=1)], axis=0
    )
    step_b = np.concatenate(two_terms(table), axis=0)
    sign = np.where(k1 % 2 == 0, 1.0, -1.0)[:, None] / math.sqrt(NF)
    angle_t = 2 * np.pi * np.outer(k1, j1) / NF
    twiddle = np.concatenate([sign * np.cos(angle_t), sign * np.sin(angle_t)], axis=0)
    angle_a = 2 * np.pi * np.outer(np.arange(COARSE), k1) / COARSE
    blocks = np.zeros((COARSE, block_rows, 2, block_rows, COARSE))
    for b in range(block_rows):
        blocks[:, b, 0, b, :] = np.cos(angle_a)
        blocks[:, b, 1, b, :] = -np.sin(angle_a)
    high, low = two_terms(blocks.reshape(COARSE * block_rows, 2 * block_rows * COARSE))
    step_a = np.concatenate([high, high, low], axis=1)
    return step_b, twiddle.astype(np.float32), step_a


def split_terms(values):
    high = values.astype(jnp.bfloat16)
    low = (values - high.astype(jnp.float32)).astype(jnp.bfloat16)
    return high, low


def spectra_kernel(sizes, a_count, *refs):
    half = (len(refs) - 6) // 2
    sources, places = refs[:half], refs[half + 2 : 2 * half + 2]
    out_ref, wanted_ref = refs[half : half + 2]
    chunks, padded, row_of, arrived = refs[2 * half + 2 :]
    raw_ref, offsets_ref, taps_ref, ids_ref, table_ref, step_a_ref, twiddle_ref, step_b_ref, band_ref = places
    copies = [
        pltpu.make_async_copy(source, place, arrived.at[q])
        for q, (source, place) in enumerate(zip(sources, places))
    ]
    for copy in copies:
        copy.start()
    wait_raw, wait_offsets, wait_taps, wait_ids, wait_table, wait_a, wait_t, wait_b, wait_band = [
        copy.wait for copy in copies
    ]
    rows = raw_ref.shape[0]
    windows = offsets_ref.shape[0]
    count = rows * windows
    chunk_total = raw_ref.shape[1] // LANES
    padded[...] = jnp.zeros_like(padded)
    wait_taps()
    padded[0:1, 0:TAPS] = taps_ref[...]
    plain = jnp.broadcast_to(padded[0:1, :], padded.shape)
    sublane = lax.broadcasted_iota(jnp.int32, padded.shape, 0)
    stair = plain
    for i in range(1, 8):
        stair = jnp.where(sublane == i, pltpu.roll(plain, DEC * i, 1), stair)
    stair = jnp.concatenate([stair, jnp.zeros((8, 2 * LANES), jnp.float32)], axis=1)
    empty = jnp.zeros((GRAIN, LANES), jnp.float32)
    wait_offsets()
    starts, filters = [], []
    for w in range(windows):
        start = offsets_ref[w]
        first = jnp.minimum(start // LANES, chunk_total - WINDOW_CHUNKS)
        shift = start - first * LANES
        starts.append(pl.multiple_of(first * LANES, LANES))
        band = jnp.concatenate(
            [pltpu.roll(stair, shift + 8 * DEC * g, 1) for g in range(GRAIN // 8)], axis=0
        )
        columns = []
        for m in range(6):
            column = [
                band[:, (m - g) * LANES : (m - g + 1) * LANES] if 0 <= m - g < 3 else empty
                for g in range(DEC)
            ]
            columns.append(jnp.concatenate(column, axis=0))
        filters.append(jnp.concatenate(split_terms(jnp.concatenate(columns, axis=1)), axis=0))
    for wait in (wait_raw, wait_ids, wait_table, wait_a, wait_t, wait_b, wait_band):
        wait()
    parts = []
    for w in range(windows):
        slab = raw_ref[:, pl.ds(starts[w], WINDOW_CHUNKS * LANES)].astype(jnp.float32)
        for c in range(WINDOW_CHUNKS):
            chunks[w, rows * c : rows * (c + 1), :] = slab[:, c * LANES : (c + 1) * LANES]
        left = []
        for m in range(6):
            pieces = [
                chunks[w, pl.ds(rows * m + r, COARSE, stride=rows * CHUNK_STEP), :] for r in range(rows)
            ]
            left.append(jnp.concatenate(pieces, axis=0).astype(jnp.bfloat16))
        both = lax.dot_general(
            jnp.concatenate(left, axis=1),
            filters[w],
            (((1,), (1,)), ((), ())),
            preferred_element_type=jnp.float32,
        )
        parts.append((both[:, :LANES] + both[:, LANES:]).astype(jnp.bfloat16))
    decimated = jnp.concatenate(parts, axis=0)
    pairs, _, subs = sizes
    channels = ids_ref.shape[0]
    slots = table_ref.shape[1] // pairs
    block_rows = a_count * sizes[1] * subs
    my_pair = lax.axis_index("pairs")
    first_a = (lax.axis_index("section") * subs + lax.axis_index("sub")) * a_count
    for c in range(channels):
        row_of[ids_ref[c]] = c
    width = 1 + a_count + block_rows
    for s in range(slots):
        first_block = table_ref[0, my_pair * slots + s]
        second_block = table_ref[1, my_pair * slots + s]
        wanted_ref[s * width] = first_block
        first_block = jnp.maximum(first_block, 0) * block_rows + first_a
        second_block = jnp.maximum(second_block, 0) * block_rows
        for a in range(a_count):
            wanted_ref[s * width + 1 + a] = row_of[first_block + a]
        for b in range(block_rows):
            wanted_ref[s * width + 1 + a_count + b] = row_of[second_block + b]
    coarse = jnp.dot(
        step_a_ref[...], jnp.concatenate([decimated, decimated], axis=0), preferred_element_type=jnp.float32
    )
    size = count * COARSE
    real = coarse[:size].reshape(count, COARSE, LANES)
    imag = coarse[size:].reshape(count, COARSE, LANES)
    cos_t = twiddle_ref[:COARSE][None]
    sin_t = twiddle_ref[COARSE:][None]
    turned = jnp.concatenate(
        [
            (real * cos_t - imag * sin_t).reshape(size, LANES),
            (real * sin_t + imag * cos_t).reshape(size, LANES),
        ],
        axis=1,
    )
    high, low = split_terms(turned)
    spectrum = jnp.dot(
        jnp.concatenate([high, low, high], axis=1), step_b_ref[...], preferred_element_type=jnp.float32
    ).reshape(count, COARSE, LANES)
    power = jnp.sum(spectrum * spectrum, axis=1)
    high, low = split_terms(power)
    banded = jnp.dot(high, band_ref[...], preferred_element_type=jnp.float32) + jnp.dot(
        low, band_ref[...], preferred_element_type=jnp.float32
    )
    inverse_rms = lax.rsqrt(banded * (1.0 / BAND) + 1e-06)
    out_ref[...] = (spectrum * inverse_rms[:, None, :]).reshape(size, LANES).astype(jnp.bfloat16)


def correlate_kernel(
    plan, groups_of, wanted_ref, step_b_ref, twiddle_ref, step_a_ref, *refs
):
    piece_refs = refs[: len(plan)]
    out_ref, gathered, staged, sent = refs[len(plan) :]
    pairs, sections, subs = groups_of
    a_count, slots, block_rows = staged.shape[:3]
    rows_total, windows_total = gathered.shape[:2]
    rows = rows_total // (pairs * sections)
    windows = windows_total // subs
    tile = rows * windows * COARSE
    my_pair = lax.axis_index("pairs")
    my_section = lax.axis_index("section")
    my_sub = lax.axis_index("sub")

    for ref, blocks in zip(piece_refs, plan):
        for q, (locate, offset) in enumerate(blocks):
            pair, section, sub = locate(my_pair, my_section, my_sub)
            base_row = (pair * sections + section) * rows
            base_window = sub * windows
            for r in range(rows):
                for w in range(windows):
                    at = offset + (r * windows + w) * COARSE
                    gathered[base_row + r, base_window + w] = ref[at : at + COARSE, :]

    lane = lax.broadcasted_iota(jnp.int32, (COARSE, LANES), 1)
    coarse_bin = lax.broadcasted_iota(jnp.int32, (COARSE, LANES), 0)
    in_left = lane < HALF
    is_zero_bin = (coarse_bin == 0) & (lane % HALF == 0)
    weight = jnp.where(is_zero_bin, 1.0, 2.0) * (1.0 / windows_total)
    cos_t = twiddle_ref[:COARSE][None]
    sin_t = twiddle_ref[COARSE:][None]
    size = block_rows * COARSE
    width = 1 + a_count + block_rows

    def write_out(s):
        return pltpu.make_async_copy(staged.at[:, s], out_ref.at[:, s], sent.at[s])

    def one_slot(s, carry):
        live = jnp.where(wanted_ref[s * width] >= 0, 1.0, 0.0)
        scale = weight * live
        ones, turns = [], []
        for a in range(a_count):
            row = wanted_ref[s * width + 1 + a]
            one = [gathered[row, w].astype(jnp.float32) for w in range(windows_total)]
            ones.append(one)
            turns.append([jnp.where(in_left, 1.0, -1.0) * pltpu.roll(v, HALF, 1) for v in one])
        crosses = [[] for _ in range(a_count)]
        for b in range(block_rows):
            row = wanted_ref[s * width + 1 + a_count + b]
            other = [gathered[row, w].astype(jnp.float32) for w in range(windows_total)]
            for a in range(a_count):
                even = ones[a][0] * other[0]
                odd = turns[a][0] * other[0]
                for w in range(1, windows_total):
                    even = even + ones[a][w] * other[w]
                    odd = odd + turns[a][w] * other[w]
                cross = jnp.where(in_left, even, odd) + pltpu.roll(jnp.where(in_left, odd, even), HALF, 1)
                crosses[a].append((cross * scale).astype(jnp.bfloat16))
        cross = jnp.concatenate([c for per_a in crosses for c in per_a], axis=0)
        fine = jnp.dot(
            jnp.concatenate([cross, cross], axis=1), step_b_ref[...], preferred_element_type=jnp.float32
        ).reshape(a_count * block_rows, COARSE, 2 * LANES)
        real, imag = fine[:, :, :LANES], fine[:, :, LANES:]
        turned_real = (real * cos_t - imag * sin_t).reshape(a_count, size, LANES)
        turned_imag = (real * sin_t + imag * cos_t).reshape(a_count, size, LANES)
        turned = jnp.concatenate(
            [
                jnp.concatenate([turned_real[a] for a in range(a_count)], axis=1),
                jnp.concatenate([turned_imag[a] for a in range(a_count)], axis=1),
            ],
            axis=0,
        )
        return turned.astype(jnp.bfloat16), None

    def finish(s, turned):
        high, low = turned
        lags = jnp.dot(
            step_a_ref[:, : 2 * size], high, preferred_element_type=jnp.float32
        )
        for a in range(a_count):
            for j2 in range(COARSE):
                staged[a, s, :, j2 * LANES : (j2 + 1) * LANES] = lags[
                    j2 * block_rows : (j2 + 1) * block_rows, a * LANES : (a + 1) * LANES
                ]
        write_out(s).start()

    def whole_slot(s, carry):
        finish(s, one_slot(s, 0))
        return carry

    if slots <= 4:
        kept = [one_slot(s, 0) for s in range(slots)]
        for s in range(slots):
            finish(s, kept[s])
    else:
        lax.fori_loop(0, slots, whole_slot, 0)
    for s in range(slots):
        write_out(s).wait()


def exchange(mine, sizes):
    pairs, sections, subs = sizes
    block = mine.shape[0]
    axes = ("pairs", "section", "sub")
    if (pairs, sections, subs) != (4, 2, 2):
        everything = lax.all_gather(mine, axes, axis=0, tiled=True)
        blocks = []
        for z in range(pairs):
            for s in range(sections):
                for x in range(subs):
                    blocks.append(
                        ((lambda p, q, u, z=z, s=s, x=x: (z, s, x)), ((z * sections + s) * subs + x) * block)
                    )
        return [everything], [blocks]

    def chips(value, *deltas):
        moves = []
        for z in range(pairs):
            for x in range(subs):
                for s in range(sections):
                    dz, dx = deltas[s % len(deltas)]
                    moves.append((((z * sections + s) * subs + x), ((z ^ dz) * sections + s) * subs + (x ^ dx)))
        return lax.ppermute(value, axes, moves)

    def cores(value):
        return lax.ppermute(value, "section", [(0, 1), (1, 0)])

    pieces = [mine]
    plan = [[((lambda p, q, u: (p, q, u)), 0)]]
    other = cores(mine)
    pieces.append(other)
    plan.append([((lambda p, q, u: (p, 1 - q, u)), 0)])
    both = jnp.concatenate([mine, other], axis=0)
    for d0, d1 in ROUNDS:
        arrived = chips(both, d0, d1)

        def here(p, q, u, d0=d0, d1=d1):
            return (p ^ jnp.where(q == 0, d0[0], d1[0]), q, u ^ jnp.where(q == 0, d0[1], d1[1]))

        def here_flip(p, q, u, here=here):
            z, s, x = here(p, q, u)
            return z, 1 - s, x

        def there(p, q, u, here=here):
            return here(p, 1 - q, u)

        def there_flip(p, q, u, there=there):
            z, s, x = there(p, q, u)
            return z, 1 - s, x

        pieces.append(arrived)
        plan.append([(here, 0), (here_flip, block)])
        if d0 != d1:
            pieces.append(cores(arrived))
            plan.append([(there, 0), (there_flip, block)])
    return pieces, plan


def body(raw_record, fir_taps, channel_ids, offsets, pair_table):
    rows = raw_record.shape[0]
    windows = offsets.shape[0]
    sizes = tuple(lax.axis_size(name) for name in ("pairs", "section", "sub"))
    pairs, sections, subs = sizes
    block_rows = rows * sections
    slots = pair_table.shape[0] // pairs
    a_count = block_rows // (sections * subs)
    vmem = pl.BlockSpec(memory_space=pltpu.VMEM)
    smem = pl.BlockSpec(memory_space=pltpu.SMEM)

    operands = [raw_record, offsets, fir_taps.reshape(1, TAPS), channel_ids, pair_table.T]
    operands += [jnp.asarray(c) for c in forward_constants(rows, windows)]
    operands = [pltpu.with_memory_space_constraint(operand, pltpu.HBM) for operand in operands]
    in_scalar = (1, 3, 4)
    wanted_count = slots * (1 + a_count + block_rows)
    whitened, wanted = pl.pallas_call(
        functools.partial(spectra_kernel, sizes, a_count),
        name="spectra",
        out_shape=(
            pltpu.VMEM((rows * windows * COARSE, LANES), jnp.bfloat16),
            pltpu.SMEM((wanted_count,), jnp.int32),
        ),
        in_specs=[pl.BlockSpec(memory_space=pltpu.HBM)] * len(operands),
        out_specs=(vmem, smem),
        scratch_shapes=[
            (pltpu.SMEM if q in in_scalar else pltpu.VMEM)(operand.shape, operand.dtype)
            for q, operand in enumerate(operands)
        ]
        + [
            pltpu.VMEM((windows, rows * WINDOW_CHUNKS, LANES), jnp.float32),
            pltpu.VMEM((8, LANES), jnp.float32),
            pltpu.SMEM(channel_ids.shape, jnp.int32),
            pltpu.SemaphoreType.DMA((len(operands),)),
        ],
        compiler_params=pltpu.CompilerParams(vmem_limit_bytes=32 * 1024 * 1024),
    )(*operands)

    pieces, plan = exchange(whitened, sizes)

    wanted = pltpu.with_memory_space_constraint(wanted, pltpu.SMEM)
    consts = [jnp.asarray(c) for c in inverse_constants(block_rows)]
    result = (a_count, slots, block_rows, NF)
    return pl.pallas_call(
        functools.partial(correlate_kernel, plan, sizes),
        name="correlate",
        out_shape=jax.ShapeDtypeStruct(result, jnp.float32),
        in_specs=[smem] + [vmem] * (3 + len(pieces)),
        out_specs=pl.BlockSpec(memory_space=pltpu.HBM),
        scratch_shapes=[
            pltpu.VMEM((rows * pairs * sections, windows * subs, COARSE, LANES), jnp.bfloat16),
            pltpu.VMEM(result, jnp.float32),
            pltpu.SemaphoreType.DMA((slots,)),
        ],
        compiler_params=pltpu.CompilerParams(vmem_limit_bytes=32 * 1024 * 1024),
    )(wanted, *consts, *pieces)


def solution(mesh):
    return jax.shard_map(
        body,
        mesh=mesh,
        in_specs=(
            P(("groups", "pairs", "section"), "sub"),
            P(),
            P("groups"),
            P(("groups", "sub")),
            P("groups", None),
        ),
        out_specs=P(("section", "sub"), ("groups", "pairs"), None, None),
        check_vma=False,
    )
```

```python
import functools
import math

import jax
import jax.numpy as jnp
import ml_dtypes
import numpy as np
from jax import lax
from jax.experimental import pallas as pl
from jax.experimental.pallas import tpu as pltpu
from jax.sharding import PartitionSpec as P

NF = 2048
TAPS = 64
DEC = 4
BAND = 64
LANES = 128
HALF = LANES // 2
COARSE = NF // LANES

CHUNK_STEP = DEC * LANES // LANES
WINDOW_CHUNKS = CHUNK_STEP * (COARSE - 1) + 6
ROUNDS = (
    ((0, 1), (1, 1)),
    ((1, 0), (1, 0)),
    ((3, 0), (3, 1)),
    ((2, 0), (2, 1)),
)
GRAIN = LANES // DEC


def two_terms(values):
    high = values.astype(ml_dtypes.bfloat16)
    low = (values - high.astype(np.float64)).astype(ml_dtypes.bfloat16)
    return high, low


def forward_constants(rows, windows):
    k1 = np.arange(COARSE)
    fine = np.arange(LANES)
    k2 = np.arange(HALF)
    angle_a = 2 * np.pi * np.outer(k1, np.arange(COARSE)) / COARSE
    count = rows * windows
    blocks = np.zeros((2, rows, windows, COARSE, windows, rows, COARSE))
    for r in range(rows):
        for w in range(windows):
            blocks[0, r, w, :, w, r, :] = np.cos(angle_a)
            blocks[1, r, w, :, w, r, :] = -np.sin(angle_a)
    high, low = two_terms(blocks.reshape(2 * count * COARSE, count * COARSE))
    step_a = np.concatenate([high, low], axis=1)
    angle_t = 2 * np.pi * np.outer(k1, fine) / NF
    twiddle = np.concatenate([np.cos(angle_t), -np.sin(angle_t)], axis=0).astype(np.float32)
    angle_b = 2 * np.pi * np.outer(fine, k2) / LANES
    cos_b, sin_b = np.cos(angle_b), np.sin(angle_b)
    table = np.concatenate(
        [np.concatenate([cos_b, -sin_b], axis=1), np.concatenate([sin_b, cos_b], axis=1)], axis=0
    )
    high, low = two_terms(table)
    step_b = np.concatenate([high, high, low], axis=0)
    band_of = np.tile(k2 * COARSE // BAND, 2)
    same_band = (band_of[:, None] == band_of[None, :]).astype(ml_dtypes.bfloat16)
    return step_a, twiddle, step_b, same_band


def inverse_constants(block_rows):
    k1 = np.arange(COARSE)
    k2 = np.arange(HALF)
    j1 = np.arange(LANES)
    angle_b = 2 * np.pi * np.outer(k2, j1) / LANES
    cos_b, sin_b = np.cos(angle_b), np.sin(angle_b)
    real_rows = np.concatenate([cos_b, sin_b], axis=1)
    imag_rows = np.concatenate([-sin_b, cos_b], axis=1)
    step_b = np.concatenate([real_rows, real_rows, imag_rows, imag_rows], axis=0).astype(ml_dtypes.bfloat16)
    sign = np.where(k1 % 2 == 0, 1.0, -1.0)[:, None] / math.sqrt(NF)
    angle_t = 2 * np.pi * np.outer(k1, j1) / NF
    twiddle = np.concatenate([sign * np.cos(angle_t), sign * np.sin(angle_t)], axis=0)
    angle_a = 2 * np.pi * np.outer(np.arange(COARSE), k1) / COARSE
    blocks = np.zeros((COARSE, block_rows, 2, block_rows, COARSE))
    for b in range(block_rows):
        blocks[:, b, 0, b, :] = np.cos(angle_a)
        blocks[:, b, 1, b, :] = -np.sin(angle_a)
    high, low = two_terms(blocks.reshape(COARSE * block_rows, 2 * block_rows * COARSE))
    step_a = np.concatenate([high, high, low], axis=1)
    return step_b, twiddle.astype(np.float32), step_a


def split_terms(values):
    high = values.astype(jnp.bfloat16)
    low = (values - high.astype(jnp.float32)).astype(jnp.bfloat16)
    return high, low


def spectra_kernel(sizes, a_count, *refs):
    half = (len(refs) - 6) // 2
    sources, places = refs[:half], refs[half + 2 : 2 * half + 2]
    out_ref, wanted_ref = refs[half : half + 2]
    chunks, padded, row_of, arrived = refs[2 * half + 2 :]
    raw_ref, offsets_ref, taps_ref, ids_ref, table_ref, step_a_ref, twiddle_ref, step_b_ref, band_ref = places
    copies = [
        pltpu.make_async_copy(source, place, arrived.at[q])
        for q, (source, place) in enumerate(zip(sources, places))
    ]
    for copy in copies:
        copy.start()
    wait_raw, wait_offsets, wait_taps, wait_ids, wait_table, wait_a, wait_t, wait_b, wait_band = [
        copy.wait for copy in copies
    ]
    rows = raw_ref.shape[0]
    windows = offsets_ref.shape[0]
    count = rows * windows
    chunk_total = raw_ref.shape[1] // LANES
    padded[...] = jnp.zeros_like(padded)
    wait_taps()
    padded[0:1, 0:TAPS] = taps_ref[...]
    plain = jnp.broadcast_to(padded[0:1, :], padded.shape)
    sublane = lax.broadcasted_iota(jnp.int32, padded.shape, 0)
    stair = plain
    for i in range(1, 8):
        stair = jnp.where(sublane == i, pltpu.roll(plain, DEC * i, 1), stair)
    stair = jnp.concatenate([stair, jnp.zeros((8, 2 * LANES), jnp.float32)], axis=1)
    empty = jnp.zeros((GRAIN, LANES), jnp.float32)
    wait_offsets()
    starts, filters = [], []
    for w in range(windows):
        start = offsets_ref[w]
        first = jnp.minimum(start // LANES, chunk_total - WINDOW_CHUNKS)
        shift = start - first * LANES
        starts.append(pl.multiple_of(first * LANES, LANES))
        band = jnp.concatenate(
            [pltpu.roll(stair, shift + 8 * DEC * g, 1) for g in range(GRAIN // 8)], axis=0
        )
        columns = []
        for m in range(6):
            column = [
                band[:, (m - g) * LANES : (m - g + 1) * LANES] if 0 <= m - g < 3 else empty
                for g in range(DEC)
            ]
            columns.append(jnp.concatenate(column, axis=0))
        filters.append(jnp.concatenate(split_terms(jnp.concatenate(columns, axis=1)), axis=0))
    for wait in (wait_raw, wait_ids, wait_table, wait_a, wait_t, wait_b, wait_band):
        wait()
    parts = []
    for w in range(windows):
        slab = raw_ref[:, pl.ds(starts[w], WINDOW_CHUNKS * LANES)].astype(jnp.float32)
        for c in range(WINDOW_CHUNKS):
            chunks[w, rows * c : rows * (c + 1), :] = slab[:, c * LANES : (c + 1) * LANES]
        left = []
        for m in range(6):
            pieces = [
                chunks[w, pl.ds(rows * m + r, COARSE, stride=rows * CHUNK_STEP), :] for r in range(rows)
            ]
            left.append(jnp.concatenate(pieces, axis=0).astype(jnp.bfloat16))
        both = lax.dot_general(
            jnp.concatenate(left, axis=1),
            filters[w],
            (((1,), (1,)), ((), ())),
            preferred_element_type=jnp.float32,
        )
        parts.append((both[:, :LANES] + both[:, LANES:]).astype(jnp.bfloat16))
    decimated = jnp.concatenate(parts, axis=0)
    pairs, _, subs = sizes
    channels = ids_ref.shape[0]
    slots = table_ref.shape[1] // pairs
    block_rows = a_count * sizes[1] * subs
    my_pair = lax.axis_index("pairs")
    first_a = (lax.axis_index("section") * subs + lax.axis_index("sub")) * a_count
    for c in range(channels):
        row_of[ids_ref[c]] = c
    width = 1 + a_count + block_rows
    for s in range(slots):
        first_block = table_ref[0, my_pair * slots + s]
        second_block = table_ref[1, my_pair * slots + s]
        wanted_ref[s * width] = first_block
        first_block = jnp.maximum(first_block, 0) * block_rows + first_a
        second_block = jnp.maximum(second_block, 0) * block_rows
        for a in range(a_count):
            wanted_ref[s * width + 1 + a] = row_of[first_block + a]
        for b in range(block_rows):
            wanted_ref[s * width + 1 + a_count + b] = row_of[second_block + b]
    coarse = jnp.dot(
        step_a_ref[...], jnp.concatenate([decimated, decimated], axis=0), preferred_element_type=jnp.float32
    )
    size = count * COARSE
    real = coarse[:size].reshape(count, COARSE, LANES)
    imag = coarse[size:].reshape(count, COARSE, LANES)
    cos_t = twiddle_ref[:COARSE][None]
    sin_t = twiddle_ref[COARSE:][None]
    turned = jnp.concatenate(
        [
            (real * cos_t - imag * sin_t).reshape(size, LANES),
            (real * sin_t + imag * cos_t).reshape(size, LANES),
        ],
        axis=1,
    )
    high, low = split_terms(turned)
    spectrum = jnp.dot(
        jnp.concatenate([high, low, high], axis=1), step_b_ref[...], preferred_element_type=jnp.float32
    ).reshape(count, COARSE, LANES)
    power = jnp.sum(spectrum * spectrum, axis=1)
    high, low = split_terms(power)
    banded = jnp.dot(high, band_ref[...], preferred_element_type=jnp.float32) + jnp.dot(
        low, band_ref[...], preferred_element_type=jnp.float32
    )
    inverse_rms = lax.rsqrt(banded * (1.0 / BAND) + 1e-06)
    out_ref[...] = (spectrum * inverse_rms[:, None, :]).reshape(size, LANES).astype(jnp.bfloat16)


def correlate_kernel(
    plan, groups_of, wanted_ref, step_b_ref, twiddle_ref, step_a_ref, *refs
):
    piece_refs = refs[: len(plan)]
    out_ref, gathered, staged, sent = refs[len(plan) :]
    pairs, sections, subs = groups_of
    a_count, slots, block_rows = staged.shape[:3]
    rows_total, windows_total = gathered.shape[:2]
    rows = rows_total // (pairs * sections)
    windows = windows_total // subs
    tile = rows * windows * COARSE
    my_pair = lax.axis_index("pairs")
    my_section = lax.axis_index("section")
    my_sub = lax.axis_index("sub")

    for ref, blocks in zip(piece_refs, plan):
        for q, (locate, offset) in enumerate(blocks):
            pair, section, sub = locate(my_pair, my_section, my_sub)
            base_row = (pair * sections + section) * rows
            base_window = sub * windows
            for r in range(rows):
                for w in range(windows):
                    at = offset + (r * windows + w) * COARSE
                    gathered[base_row + r, base_window + w] = ref[at : at + COARSE, :]

    lane = lax.broadcasted_iota(jnp.int32, (COARSE, LANES), 1)
    coarse_bin = lax.broadcasted_iota(jnp.int32, (COARSE, LANES), 0)
    in_left = lane < HALF
    is_zero_bin = (coarse_bin == 0) & (lane % HALF == 0)
    weight = jnp.where(is_zero_bin, 1.0, 2.0) * (1.0 / windows_total)
    cos_t = twiddle_ref[:COARSE][None]
    sin_t = twiddle_ref[COARSE:][None]
    size = block_rows * COARSE
    width = 1 + a_count + block_rows

    def write_out(s):
        return pltpu.make_async_copy(staged.at[:, s], out_ref.at[:, s], sent.at[s])

    def one_slot(s, carry):
        live = jnp.where(wanted_ref[s * width] >= 0, 1.0, 0.0)
        scale = weight * live
        ones, turns = [], []
        for a in range(a_count):
            row = wanted_ref[s * width + 1 + a]
            one = [gathered[row, w].astype(jnp.float32) for w in range(windows_total)]
            ones.append(one)
            turns.append([jnp.where(in_left, 1.0, -1.0) * pltpu.roll(v, HALF, 1) for v in one])
        crosses = [[] for _ in range(a_count)]
        for b in range(block_rows):
            row = wanted_ref[s * width + 1 + a_count + b]
            other = [gathered[row, w].astype(jnp.float32) for w in range(windows_total)]
            for a in range(a_count):
                even = ones[a][0] * other[0]
                odd = turns[a][0] * other[0]
                for w in range(1, windows_total):
                    even = even + ones[a][w] * other[w]
                    odd = odd + turns[a][w] * other[w]
                cross = jnp.concatenate([even * scale, odd * scale], axis=1)
                crosses[a].append(cross.astype(jnp.bfloat16))
        cross = jnp.concatenate([c for per_a in crosses for c in per_a], axis=0)
        fine = jnp.dot(
            cross, step_b_ref[...], preferred_element_type=jnp.float32
        ).reshape(a_count * block_rows, COARSE, 2 * LANES)
        real, imag = fine[:, :, :LANES], fine[:, :, LANES:]
        turned_real = (real * cos_t - imag * sin_t).reshape(a_count, size, LANES)
        turned_imag = (real * sin_t + imag * cos_t).reshape(a_count, size, LANES)
        turned = jnp.concatenate(
            [
                jnp.concatenate([turned_real[a] for a in range(a_count)], axis=1),
                jnp.concatenate([turned_imag[a] for a in range(a_count)], axis=1),
            ],
            axis=0,
        )
        return turned.astype(jnp.bfloat16), None

    def finish(s, turned):
        high, low = turned
        lags = jnp.dot(
            step_a_ref[:, : 2 * size], high, preferred_element_type=jnp.float32
        )
        for a in range(a_count):
            for j2 in range(COARSE):
                staged[a, s, :, j2 * LANES : (j2 + 1) * LANES] = lags[
                    j2 * block_rows : (j2 + 1) * block_rows, a * LANES : (a + 1) * LANES
                ]
        write_out(s).start()

    def whole_slot(s, carry):
        finish(s, one_slot(s, 0))
        return carry

    if slots <= 4:
        kept = [one_slot(s, 0) for s in range(slots)]
        for s in range(slots):
            finish(s, kept[s])
    else:
        lax.fori_loop(0, slots, whole_slot, 0)
    for s in range(slots):
        write_out(s).wait()


def exchange(mine, sizes):
    pairs, sections, subs = sizes
    block = mine.shape[0]
    axes = ("pairs", "section", "sub")
    if (pairs, sections, subs) != (4, 2, 2):
        everything = lax.all_gather(mine, axes, axis=0, tiled=True)
        blocks = []
        for z in range(pairs):
            for s in range(sections):
                for x in range(subs):
                    blocks.append(
                        ((lambda p, q, u, z=z, s=s, x=x: (z, s, x)), ((z * sections + s) * subs + x) * block)
                    )
        return [everything], [blocks]

    def chips(value, *deltas):
        moves = []
        for z in range(pairs):
            for x in range(subs):
                for s in range(sections):
                    dz, dx = deltas[s % len(deltas)]
                    moves.append((((z * sections + s) * subs + x), ((z ^ dz) * sections + s) * subs + (x ^ dx)))
        return lax.ppermute(value, axes, moves)

    def cores(value):
        return lax.ppermute(value, "section", [(0, 1), (1, 0)])

    pieces = [mine]
    plan = [[((lambda p, q, u: (p, q, u)), 0)]]
    other = cores(mine)
    pieces.append(other)
    plan.append([((lambda p, q, u: (p, 1 - q, u)), 0)])
    both = jnp.concatenate([mine, other], axis=0)
    for d0, d1 in ROUNDS:
        arrived = chips(both, d0, d1)

        def here(p, q, u, d0=d0, d1=d1):
            return (p ^ jnp.where(q == 0, d0[0], d1[0]), q, u ^ jnp.where(q == 0, d0[1], d1[1]))

        def here_flip(p, q, u, here=here):
            z, s, x = here(p, q, u)
            return z, 1 - s, x

        def there(p, q, u, here=here):
            return here(p, 1 - q, u)

        def there_flip(p, q, u, there=there):
            z, s, x = there(p, q, u)
            return z, 1 - s, x

        pieces.append(arrived)
        plan.append([(here, 0), (here_flip, block)])
        if d0 != d1:
            pieces.append(cores(arrived))
            plan.append([(there, 0), (there_flip, block)])
    return pieces, plan


def body(raw_record, fir_taps, channel_ids, offsets, pair_table):
    rows = raw_record.shape[0]
    windows = offsets.shape[0]
    sizes = tuple(lax.axis_size(name) for name in ("pairs", "section", "sub"))
    pairs, sections, subs = sizes
    block_rows = rows * sections
    slots = pair_table.shape[0] // pairs
    a_count = block_rows // (sections * subs)
    vmem = pl.BlockSpec(memory_space=pltpu.VMEM)
    smem = pl.BlockSpec(memory_space=pltpu.SMEM)

    operands = [raw_record, offsets, fir_taps.reshape(1, TAPS), channel_ids, pair_table.T]
    operands += [jnp.asarray(c) for c in forward_constants(rows, windows)]
    operands = [pltpu.with_memory_space_constraint(operand, pltpu.HBM) for operand in operands]
    in_scalar = (1, 3, 4)
    wanted_count = slots * (1 + a_count + block_rows)
    whitened, wanted = pl.pallas_call(
        functools.partial(spectra_kernel, sizes, a_count),
        name="spectra",
        out_shape=(
            pltpu.VMEM((rows * windows * COARSE, LANES), jnp.bfloat16),
            pltpu.SMEM((wanted_count,), jnp.int32),
        ),
        in_specs=[pl.BlockSpec(memory_space=pltpu.HBM)] * len(operands),
        out_specs=(vmem, smem),
        scratch_shapes=[
            (pltpu.SMEM if q in in_scalar else pltpu.VMEM)(operand.shape, operand.dtype)
            for q, operand in enumerate(operands)
        ]
        + [
            pltpu.VMEM((windows, rows * WINDOW_CHUNKS, LANES), jnp.float32),
            pltpu.VMEM((8, LANES), jnp.float32),
            pltpu.SMEM(channel_ids.shape, jnp.int32),
            pltpu.SemaphoreType.DMA((len(operands),)),
        ],
        compiler_params=pltpu.CompilerParams(vmem_limit_bytes=32 * 1024 * 1024),
    )(*operands)

    pieces, plan = exchange(whitened, sizes)

    wanted = pltpu.with_memory_space_constraint(wanted, pltpu.SMEM)
    consts = [jnp.asarray(c) for c in inverse_constants(block_rows)]
    result = (a_count, slots, block_rows, NF)
    return pl.pallas_call(
        functools.partial(correlate_kernel, plan, sizes),
        name="correlate",
        out_shape=jax.ShapeDtypeStruct(result, jnp.float32),
        in_specs=[smem] + [vmem] * (3 + len(pieces)),
        out_specs=pl.BlockSpec(memory_space=pltpu.HBM),
        scratch_shapes=[
            pltpu.VMEM((rows * pairs * sections, windows * subs, COARSE, LANES), jnp.bfloat16),
            pltpu.VMEM(result, jnp.float32),
            pltpu.SemaphoreType.DMA((slots,)),
        ],
        compiler_params=pltpu.CompilerParams(vmem_limit_bytes=32 * 1024 * 1024),
    )(wanted, *consts, *pieces)


def solution(mesh):
    return jax.shard_map(
        body,
        mesh=mesh,
        in_specs=(
            P(("groups", "pairs", "section"), "sub"),
            P(),
            P("groups"),
            P(("groups", "sub")),
            P("groups", None),
        ),
        out_specs=P(("section", "sub"), ("groups", "pairs"), None, None),
        check_vma=False,
    )
```

```python
import functools
import math

import jax
import jax.numpy as jnp
import ml_dtypes
import numpy as np
from jax import lax
from jax.experimental import pallas as pl
from jax.experimental.pallas import tpu as pltpu
from jax.sharding import PartitionSpec as P

NF = 2048
TAPS = 64
DEC = 4
BAND = 64
LANES = 128
HALF = LANES // 2
COARSE = NF // LANES

CHUNK_STEP = DEC * LANES // LANES
WINDOW_CHUNKS = CHUNK_STEP * (COARSE - 1) + 6
ROUNDS = (
    ((0, 1), (1, 1)),
    ((1, 0), (1, 0)),
    ((3, 0), (3, 1)),
    ((2, 0), (2, 1)),
)
GRAIN = LANES // DEC


def two_terms(values):
    high = values.astype(ml_dtypes.bfloat16)
    low = (values - high.astype(np.float64)).astype(ml_dtypes.bfloat16)
    return high, low


def forward_constants(rows, windows):
    k1 = np.arange(COARSE)
    fine = np.arange(LANES)
    k2 = np.arange(HALF)
    angle_a = 2 * np.pi * np.outer(k1, np.arange(COARSE)) / COARSE
    count = rows * windows
    blocks = np.zeros((2, rows, windows, COARSE, windows, rows, COARSE))
    for r in range(rows):
        for w in range(windows):
            blocks[0, r, w, :, w, r, :] = np.cos(angle_a)
            blocks[1, r, w, :, w, r, :] = -np.sin(angle_a)
    step_a = blocks.reshape(2 * count * COARSE, count * COARSE).astype(ml_dtypes.bfloat16)
    angle_t = 2 * np.pi * np.outer(k1, fine) / NF
    twiddle = np.concatenate([np.cos(angle_t), -np.sin(angle_t)], axis=0).astype(np.float32)
    angle_b = 2 * np.pi * np.outer(fine, k2) / LANES
    cos_b, sin_b = np.cos(angle_b), np.sin(angle_b)
    table = np.concatenate(
        [np.concatenate([cos_b, -sin_b], axis=1), np.concatenate([sin_b, cos_b], axis=1)], axis=0
    )
    high, low = two_terms(table)
    step_b = np.concatenate([high, high, low], axis=0)
    band_of = np.tile(k2 * COARSE // BAND, 2)
    same_band = (band_of[:, None] == band_of[None, :]).astype(ml_dtypes.bfloat16)
    return step_a, twiddle, step_b, same_band


def inverse_constants(block_rows):
    k1 = np.arange(COARSE)
    k2 = np.arange(HALF)
    j1 = np.arange(LANES)
    angle_b = 2 * np.pi * np.outer(k2, j1) / LANES
    cos_b, sin_b = np.cos(angle_b), np.sin(angle_b)
    table = np.concatenate(
        [np.concatenate([cos_b, sin_b], axis=1), np.concatenate([-sin_b, cos_b], axis=1)], axis=0
    )
    step_b = np.concatenate(two_terms(table), axis=0)
    sign = np.where(k1 % 2 == 0, 1.0, -1.0)[:, None] / math.sqrt(NF)
    angle_t = 2 * np.pi * np.outer(k1, j1) / NF
    twiddle = np.concatenate([sign * np.cos(angle_t), sign * np.sin(angle_t)], axis=0)
    angle_a = 2 * np.pi * np.outer(np.arange(COARSE), k1) / COARSE
    blocks = np.zeros((COARSE, block_rows, 2, block_rows, COARSE))
    for b in range(block_rows):
        blocks[:, b, 0, b, :] = np.cos(angle_a)
        blocks[:, b, 1, b, :] = -np.sin(angle_a)
    high, low = two_terms(blocks.reshape(COARSE * block_rows, 2 * block_rows * COARSE))
    step_a = np.concatenate([high, high, low], axis=1)
    return step_b, twiddle.astype(np.float32), step_a


def split_terms(values):
    high = values.astype(jnp.bfloat16)
    low = (values - high.astype(jnp.float32)).astype(jnp.bfloat16)
    return high, low


def spectra_kernel(sizes, a_count, *refs):
    half = (len(refs) - 6) // 2
    sources, places = refs[:half], refs[half + 2 : 2 * half + 2]
    out_ref, wanted_ref = refs[half : half + 2]
    chunks, padded, row_of, arrived = refs[2 * half + 2 :]
    raw_ref, offsets_ref, taps_ref, ids_ref, table_ref, step_a_ref, twiddle_ref, step_b_ref, band_ref = places
    copies = [
        pltpu.make_async_copy(source, place, arrived.at[q])
        for q, (source, place) in enumerate(zip(sources, places))
    ]
    for copy in copies:
        copy.start()
    wait_raw, wait_offsets, wait_taps, wait_ids, wait_table, wait_a, wait_t, wait_b, wait_band = [
        copy.wait for copy in copies
    ]
    rows = raw_ref.shape[0]
    windows = offsets_ref.shape[0]
    count = rows * windows
    chunk_total = raw_ref.shape[1] // LANES
    padded[...] = jnp.zeros_like(padded)
    wait_taps()
    padded[0:1, 0:TAPS] = taps_ref[...]
    plain = jnp.broadcast_to(padded[0:1, :], padded.shape)
    sublane = lax.broadcasted_iota(jnp.int32, padded.shape, 0)
    stair = plain
    for i in range(1, 8):
        stair = jnp.where(sublane == i, pltpu.roll(plain, DEC * i, 1), stair)
    stair = jnp.concatenate([stair, jnp.zeros((8, 2 * LANES), jnp.float32)], axis=1)
    empty = jnp.zeros((GRAIN, LANES), jnp.float32)
    wait_offsets()
    starts, filters = [], []
    for w in range(windows):
        start = offsets_ref[w]
        first = jnp.minimum(start // LANES, chunk_total - WINDOW_CHUNKS)
        shift = start - first * LANES
        starts.append(pl.multiple_of(first * LANES, LANES))
        band = jnp.concatenate(
            [pltpu.roll(stair, shift + 8 * DEC * g, 1) for g in range(GRAIN // 8)], axis=0
        )
        columns = []
        for m in range(6):
            column = [
                band[:, (m - g) * LANES : (m - g + 1) * LANES] if 0 <= m - g < 3 else empty
                for g in range(DEC)
            ]
            columns.append(jnp.concatenate(column, axis=0))
        filters.append(jnp.concatenate(split_terms(jnp.concatenate(columns, axis=1)), axis=0))
    for wait in (wait_raw, wait_ids, wait_table, wait_a, wait_t, wait_b, wait_band):
        wait()
    parts = []
    for w in range(windows):
        slab = raw_ref[:, pl.ds(starts[w], WINDOW_CHUNKS * LANES)].astype(jnp.float32)
        for c in range(WINDOW_CHUNKS):
            chunks[w, rows * c : rows * (c + 1), :] = slab[:, c * LANES : (c + 1) * LANES]
        left = []
        for m in range(6):
            pieces = [
                chunks[w, pl.ds(rows * m + r, COARSE, stride=rows * CHUNK_STEP), :] for r in range(rows)
            ]
            left.append(jnp.concatenate(pieces, axis=0).astype(jnp.bfloat16))
        both = lax.dot_general(
            jnp.concatenate(left, axis=1),
            filters[w],
            (((1,), (1,)), ((), ())),
            preferred_element_type=jnp.float32,
        )
        parts.append((both[:, :LANES] + both[:, LANES:]).astype(jnp.bfloat16))
    decimated = jnp.concatenate(parts, axis=0)
    pairs, _, subs = sizes
    channels = ids_ref.shape[0]
    slots = table_ref.shape[1] // pairs
    block_rows = a_count * sizes[1] * subs
    my_pair = lax.axis_index("pairs")
    first_a = (lax.axis_index("section") * subs + lax.axis_index("sub")) * a_count
    for c in range(channels):
        row_of[ids_ref[c]] = c
    width = 1 + a_count + block_rows
    for s in range(slots):
        first_block = table_ref[0, my_pair * slots + s]
        second_block = table_ref[1, my_pair * slots + s]
        wanted_ref[s * width] = first_block
        first_block = jnp.maximum(first_block, 0) * block_rows + first_a
        second_block = jnp.maximum(second_block, 0) * block_rows
        for a in range(a_count):
            wanted_ref[s * width + 1 + a] = row_of[first_block + a]
        for b in range(block_rows):
            wanted_ref[s * width + 1 + a_count + b] = row_of[second_block + b]
    coarse = jnp.dot(
        step_a_ref[...], decimated, preferred_element_type=jnp.float32
    )
    size = count * COARSE
    real = coarse[:size].reshape(count, COARSE, LANES)
    imag = coarse[size:].reshape(count, COARSE, LANES)
    cos_t = twiddle_ref[:COARSE][None]
    sin_t = twiddle_ref[COARSE:][None]
    turned = jnp.concatenate(
        [
            (real * cos_t - imag * sin_t).reshape(size, LANES),
            (real * sin_t + imag * cos_t).reshape(size, LANES),
        ],
        axis=1,
    )
    high, low = split_terms(turned)
    spectrum = jnp.dot(
        jnp.concatenate([high, low, high], axis=1), step_b_ref[...], preferred_element_type=jnp.float32
    ).reshape(count, COARSE, LANES)
    power = jnp.sum(spectrum * spectrum, axis=1)
    high, low = split_terms(power)
    banded = jnp.dot(high, band_ref[...], preferred_element_type=jnp.float32) + jnp.dot(
        low, band_ref[...], preferred_element_type=jnp.float32
    )
    inverse_rms = lax.rsqrt(banded * (1.0 / BAND) + 1e-06)
    out_ref[...] = (spectrum * inverse_rms[:, None, :]).reshape(size, LANES).astype(jnp.bfloat16)


def correlate_kernel(
    plan, groups_of, wanted_ref, step_b_ref, twiddle_ref, step_a_ref, *refs
):
    piece_refs = refs[: len(plan)]
    out_ref, gathered, staged, sent = refs[len(plan) :]
    pairs, sections, subs = groups_of
    a_count, slots, block_rows = staged.shape[:3]
    rows_total, windows_total = gathered.shape[:2]
    rows = rows_total // (pairs * sections)
    windows = windows_total // subs
    tile = rows * windows * COARSE
    my_pair = lax.axis_index("pairs")
    my_section = lax.axis_index("section")
    my_sub = lax.axis_index("sub")

    for ref, blocks in zip(piece_refs, plan):
        for q, (locate, offset) in enumerate(blocks):
            pair, section, sub = locate(my_pair, my_section, my_sub)
            base_row = (pair * sections + section) * rows
            base_window = sub * windows
            for r in range(rows):
                for w in range(windows):
                    at = offset + (r * windows + w) * COARSE
                    gathered[base_row + r, base_window + w] = ref[at : at + COARSE, :]

    lane = lax.broadcasted_iota(jnp.int32, (COARSE, LANES), 1)
    coarse_bin = lax.broadcasted_iota(jnp.int32, (COARSE, LANES), 0)
    in_left = lane < HALF
    is_zero_bin = (coarse_bin == 0) & (lane % HALF == 0)
    weight = jnp.where(is_zero_bin, 1.0, 2.0) * (1.0 / windows_total)
    cos_t = twiddle_ref[:COARSE][None]
    sin_t = twiddle_ref[COARSE:][None]
    size = block_rows * COARSE
    width = 1 + a_count + block_rows

    def write_out(s):
        return pltpu.make_async_copy(staged.at[:, s], out_ref.at[:, s], sent.at[s])

    def one_slot(s, carry):
        live = jnp.where(wanted_ref[s * width] >= 0, 1.0, 0.0)
        scale = weight * live
        ones, turns = [], []
        for a in range(a_count):
            row = wanted_ref[s * width + 1 + a]
            one = [gathered[row, w].astype(jnp.float32) for w in range(windows_total)]
            ones.append(one)
            turns.append([jnp.where(in_left, 1.0, -1.0) * pltpu.roll(v, HALF, 1) for v in one])
        crosses = [[] for _ in range(a_count)]
        for b in range(block_rows):
            row = wanted_ref[s * width + 1 + a_count + b]
            other = [gathered[row, w].astype(jnp.float32) for w in range(windows_total)]
            for a in range(a_count):
                even = ones[a][0] * other[0]
                odd = turns[a][0] * other[0]
                for w in range(1, windows_total):
                    even = even + ones[a][w] * other[w]
                    odd = odd + turns[a][w] * other[w]
                cross = jnp.where(in_left, even, odd) + pltpu.roll(jnp.where(in_left, odd, even), HALF, 1)
                crosses[a].append((cross * scale).astype(jnp.bfloat16))
        cross = jnp.concatenate([c for per_a in crosses for c in per_a], axis=0)
        fine = jnp.dot(
            jnp.concatenate([cross, cross], axis=1), step_b_ref[...], preferred_element_type=jnp.float32
        ).reshape(a_count * block_rows, COARSE, 2 * LANES)
        real, imag = fine[:, :, :LANES], fine[:, :, LANES:]
        turned_real = (real * cos_t - imag * sin_t).reshape(a_count, size, LANES)
        turned_imag = (real * sin_t + imag * cos_t).reshape(a_count, size, LANES)
        turned = jnp.concatenate(
            [
                jnp.concatenate([turned_real[a] for a in range(a_count)], axis=1),
                jnp.concatenate([turned_imag[a] for a in range(a_count)], axis=1),
            ],
            axis=0,
        )
        return turned.astype(jnp.bfloat16), None

    def finish(s, turned):
        high, low = turned
        lags = jnp.dot(
            step_a_ref[:, : 2 * size], high, preferred_element_type=jnp.float32
        )
        for a in range(a_count):
            for j2 in range(COARSE):
                staged[a, s, :, j2 * LANES : (j2 + 1) * LANES] = lags[
                    j2 * block_rows : (j2 + 1) * block_rows, a * LANES : (a + 1) * LANES
                ]
        write_out(s).start()

    def whole_slot(s, carry):
        finish(s, one_slot(s, 0))
        return carry

    if slots <= 4:
        kept = [one_slot(s, 0) for s in range(slots)]
        for s in range(slots):
            finish(s, kept[s])
    else:
        lax.fori_loop(0, slots, whole_slot, 0)
    for s in range(slots):
        write_out(s).wait()


def exchange(mine, sizes):
    pairs, sections, subs = sizes
    block = mine.shape[0]
    axes = ("pairs", "section", "sub")
    if (pairs, sections, subs) != (4, 2, 2):
        everything = lax.all_gather(mine, axes, axis=0, tiled=True)
        blocks = []
        for z in range(pairs):
            for s in range(sections):
                for x in range(subs):
                    blocks.append(
                        ((lambda p, q, u, z=z, s=s, x=x: (z, s, x)), ((z * sections + s) * subs + x) * block)
                    )
        return [everything], [blocks]

    def chips(value, *deltas):
        moves = []
        for z in range(pairs):
            for x in range(subs):
                for s in range(sections):
                    dz, dx = deltas[s % len(deltas)]
                    moves.append((((z * sections + s) * subs + x), ((z ^ dz) * sections + s) * subs + (x ^ dx)))
        return lax.ppermute(value, axes, moves)

    def cores(value):
        return lax.ppermute(value, "section", [(0, 1), (1, 0)])

    pieces = [mine]
    plan = [[((lambda p, q, u: (p, q, u)), 0)]]
    other = cores(mine)
    pieces.append(other)
    plan.append([((lambda p, q, u: (p, 1 - q, u)), 0)])
    both = jnp.concatenate([mine, other], axis=0)
    for d0, d1 in ROUNDS:
        arrived = chips(both, d0, d1)

        def here(p, q, u, d0=d0, d1=d1):
            return (p ^ jnp.where(q == 0, d0[0], d1[0]), q, u ^ jnp.where(q == 0, d0[1], d1[1]))

        def here_flip(p, q, u, here=here):
            z, s, x = here(p, q, u)
            return z, 1 - s, x

        def there(p, q, u, here=here):
            return here(p, 1 - q, u)

        def there_flip(p, q, u, there=there):
            z, s, x = there(p, q, u)
            return z, 1 - s, x

        pieces.append(arrived)
        plan.append([(here, 0), (here_flip, block)])
        if d0 != d1:
            pieces.append(cores(arrived))
            plan.append([(there, 0), (there_flip, block)])
    return pieces, plan


def body(raw_record, fir_taps, channel_ids, offsets, pair_table):
    rows = raw_record.shape[0]
    windows = offsets.shape[0]
    sizes = tuple(lax.axis_size(name) for name in ("pairs", "section", "sub"))
    pairs, sections, subs = sizes
    block_rows = rows * sections
    slots = pair_table.shape[0] // pairs
    a_count = block_rows // (sections * subs)
    vmem = pl.BlockSpec(memory_space=pltpu.VMEM)
    smem = pl.BlockSpec(memory_space=pltpu.SMEM)

    operands = [raw_record, offsets, fir_taps.reshape(1, TAPS), channel_ids, pair_table.T]
    operands += [jnp.asarray(c) for c in forward_constants(rows, windows)]
    operands = [pltpu.with_memory_space_constraint(operand, pltpu.HBM) for operand in operands]
    in_scalar = (1, 3, 4)
    wanted_count = slots * (1 + a_count + block_rows)
    whitened, wanted = pl.pallas_call(
        functools.partial(spectra_kernel, sizes, a_count),
        name="spectra",
        out_shape=(
            pltpu.VMEM((rows * windows * COARSE, LANES), jnp.bfloat16),
            pltpu.SMEM((wanted_count,), jnp.int32),
        ),
        in_specs=[pl.BlockSpec(memory_space=pltpu.HBM)] * len(operands),
        out_specs=(vmem, smem),
        scratch_shapes=[
            (pltpu.SMEM if q in in_scalar else pltpu.VMEM)(operand.shape, operand.dtype)
            for q, operand in enumerate(operands)
        ]
        + [
            pltpu.VMEM((windows, rows * WINDOW_CHUNKS, LANES), jnp.float32),
            pltpu.VMEM((8, LANES), jnp.float32),
            pltpu.SMEM(channel_ids.shape, jnp.int32),
            pltpu.SemaphoreType.DMA((len(operands),)),
        ],
        compiler_params=pltpu.CompilerParams(vmem_limit_bytes=32 * 1024 * 1024),
    )(*operands)

    pieces, plan = exchange(whitened, sizes)

    wanted = pltpu.with_memory_space_constraint(wanted, pltpu.SMEM)
    consts = [jnp.asarray(c) for c in inverse_constants(block_rows)]
    result = (a_count, slots, block_rows, NF)
    return pl.pallas_call(
        functools.partial(correlate_kernel, plan, sizes),
        name="correlate",
        out_shape=jax.ShapeDtypeStruct(result, jnp.float32),
        in_specs=[smem] + [vmem] * (3 + len(pieces)),
        out_specs=pl.BlockSpec(memory_space=pltpu.HBM),
        scratch_shapes=[
            pltpu.VMEM((rows * pairs * sections, windows * subs, COARSE, LANES), jnp.bfloat16),
            pltpu.VMEM(result, jnp.float32),
            pltpu.SemaphoreType.DMA((slots,)),
        ],
        compiler_params=pltpu.CompilerParams(vmem_limit_bytes=32 * 1024 * 1024),
    )(wanted, *consts, *pieces)


def solution(mesh):
    return jax.shard_map(
        body,
        mesh=mesh,
        in_specs=(
            P(("groups", "pairs", "section"), "sub"),
            P(),
            P("groups"),
            P(("groups", "sub")),
            P("groups", None),
        ),
        out_specs=P(("section", "sub"), ("groups", "pairs"), None, None),
        check_vma=False,
    )
```
